256 devices in a mesh: segment: 4 (over x_hi, core), space: 64 (over z, y, x_lo).
Axes of the slice: x: 4 (x_hi: 2, x_lo: 2; x = x_hi * 2 + x_lo), y: 4, z: 8, core: 2. Of those that a mesh axis runs over, the one named last changes fastest.
Arguments:
- clean_frames: float32 [2, 4096, 64], P(None, 'space'), may hold values from -6 to 6
- noise: float32 [2, 4096, 64], P(None, 'space'), may hold values from -6 to 6
- noise_steps: int32 [2], replicated, may hold values from 0 to 999
- noise_freqs: float32 [128], replicated, may hold values from -4 to 4
- cond_weights: bfloat16 [4, 256, 1024], P('segment'), may hold values from -0.375 to 0.375
- patch_in: float32 [16, 1024], replicated, may hold values from -1.5 to 1.5
- patch_out: bfloat16 [1024, 16], replicated, may hold values from -0.1875 to 0.1875
- section_weights: bfloat16 [4, 6144, 1024], P('segment'), may hold values from -0.1875 to 0.1875
- head_scales: float32 [4, 24], P('segment'), may hold values from 1.5 to 10
- fine_links: int32 [128, 2, 9], P('space'), may hold values from 0 to 1, as said below
- coarse_links: int32 [64, 1, 9], P('space'), may hold values from 0 to 1, as said below
Outputs:
- prediction: float32 [2, 4096, 64], P(None, 'space', 'segment')
The draws below stay inside these ranges and needn't reach their ends.
Inputs may be any that keep to these rules, and one draw needn't show every extreme that they name: `fine_links`: entry 3 (dy + 1) + (dx + 1) is 1 where the tile attends to the tile dy tile rows down and dx tile columns right: always for the tile itself, never for a tile outside the grid. `coarse_links`: entry 3 (dy + 1) + (dx + 1) is 1 where the tile attends to the tile dy tile rows down and dx tile columns right: always for the tile itself, never for a tile outside the grid.
All inputs are finite; a program needn't handle non-finite values.
Results may differ from the reference program's by a relative error of at most 0.019.
Values may be sent and summed in bfloat16 or wider, within the bound.
A program may use at most 192 MiB of HBM per device.

```python
import math
import jax
import jax.numpy as jnp
from jax import lax

D = 1024
HS = 64
H0 = 8
NF = 128
PP = 16
STEPS = 1000
MB = 2
H1 = 24
WROWS = 6144
FR = 4096
FC = 64
TR0 = 128
TC0 = 2
TR1 = 64
TC1 = 1
N_SEGMENT = 4


def neighbour_table(key, tile_rows, tile_cols):
    kept_pairs = jax.random.randint(key, (tile_rows, tile_cols, 9), 0, 4) > 0
    row_ids = jnp.arange(tile_rows)[:, None, None]
    col_ids = jnp.arange(tile_cols)[None, :, None]
    neighbour = jnp.arange(9)[None, None, :]
    row_step = neighbour // 3 - 1
    col_step = neighbour % 3 - 1
    inside = (row_ids + row_step >= 0) & (row_ids + row_step < tile_rows) & (col_ids + col_step >= 0) & (col_ids + col_step < tile_cols)
    linked = (kept_pairs | (neighbour == 4)) & inside
    return linked.astype(jnp.int32)


def draw_fine_links(key, part):
    key = jax.random.fold_in(key, 11)
    return neighbour_table(key, TR0, TC0)


def draw_coarse_links(key, part):
    key = jax.random.fold_in(key, 23)
    return neighbour_table(key, TR1, TC1)


def shard_levels(rng, dims, pieces, smallest, top_value):
    loudness = 1.0
    for axis_at, shards_of in pieces:
        heights = jax.random.uniform(jax.random.fold_in(jax.random.fold_in(rng, 6), axis_at), (shards_of,), jnp.float32, smallest / len(pieces), top_value / len(pieces))
        loudness = loudness * jnp.repeat(jnp.exp(heights), dims[axis_at] // shards_of).reshape((-1,) + (1,) * (len(dims) - 1 - axis_at))
    return loudness


def centred(key, dims, spread, reach, split=(), dtype=jnp.bfloat16):
    values = jax.random.normal(key, dims, jnp.float32) * spread
    if len(split) > 0:
        values = shard_levels(key, dims, split, -0.22, 0.18) * values
    return jnp.clip(values, min=-reach, max=reach).astype(dtype)


def setup_inputs(seed: int = 0) -> dict:
    splits = jax.random.split(jax.random.key(seed), 12)
    clean_frames = centred(splits[0], (MB, FR, FC), 1.0, 6.0, ((1, 64),), jnp.float32)
    noise = centred(splits[1], (MB, FR, FC), 1.0, 6.0, ((1, 64),), jnp.float32)
    noise_steps = jax.random.randint(splits[2], (MB,), 0, STEPS).astype(jnp.int32)
    noise_freqs = centred(splits[3], (NF,), 1.0, 4.0, (), jnp.float32)
    cond_weights = centred(splits[4], (N_SEGMENT, 2 * NF, D), (2 * NF) ** -0.5, 0.375, ((0, 4),))
    patch_in = centred(splits[5], (PP, D), PP ** -0.5, 1.5, (), jnp.float32)
    patch_out = centred(splits[6], (D, PP), D ** -0.5, 0.1875)
    section_weights = centred(splits[7], (N_SEGMENT, WROWS, D), D ** -0.5, 0.1875, ((0, 4),))
    head_scales = jnp.clip(jnp.exp(math.log(10.0) - 1.89712 * jax.random.uniform(splits[8], (N_SEGMENT, H1), jnp.float32) ** shard_levels(splits[8], (N_SEGMENT, H1), ((0, 4),), -0.2, 0.2)), 1.5, 10.0)
    fine_links = draw_fine_links(jax.random.fold_in(splits[11], 71), 0)
    coarse_links = draw_coarse_links(jax.random.fold_in(splits[11], 71), 0)
    return dict(clean_frames=clean_frames, noise=noise, noise_steps=noise_steps, noise_freqs=noise_freqs, cond_weights=cond_weights, patch_in=patch_in, patch_out=patch_out, section_weights=section_weights, head_scales=head_scales, fine_links=fine_links, coarse_links=coarse_links)


LOG_LOW = math.log(0.002)
LOG_HIGH = math.log(80.0)

def window_tables():
    query_row = jnp.arange(64) // 8
    query_col = jnp.arange(64) % 8
    key_row = jnp.arange(196) // 14
    key_col = jnp.arange(196) % 14
    inside = (jnp.abs(key_row[None, :] - 3 - query_row[:, None]) <= 3) & (jnp.abs(key_col[None, :] - 3 - query_col[:, None]) <= 3)
    row_step = (key_row >= 3).astype(jnp.int32) + (key_row >= 11).astype(jnp.int32)
    col_step = (key_col >= 3).astype(jnp.int32) + (key_col >= 11).astype(jnp.int32)
    pickers = (jnp.arange(9)[:, None] == (3 * row_step + col_step)[None, :]).astype(jnp.float32)
    return (inside.astype(jnp.float32), pickers)

def rms_rows(stream):
    return stream * lax.rsqrt(lax.optimization_barrier(jnp.mean(stream * stream, axis=-1, keepdims=True)) + 1e-06)

def unit_heads(values, head_width):
    shaped = values.reshape(values.shape[:-1] + (values.shape[-1] // head_width, head_width))
    return rms_rows(shaped).reshape(values.shape)

def attention(queries, key_values, tile_links, scales):
    row_count, col_count, inner_width = queries.shape
    head_count = scales.shape[0]
    head_width = inner_width // head_count
    tile_cols = col_count // 8
    padded = jnp.pad(key_values, ((3, 3), (3, 3), (0, 0)))
    window, pickers = window_tables()

    def one_row(tile_row):
        first_row = (tile_row * 8).astype(jnp.int32)
        query_rows = lax.dynamic_slice_in_dim(queries, first_row, 8, 0)
        band_rows = lax.dynamic_slice_in_dim(padded, first_row, 14, 0)
        query_tiles = query_rows.reshape(8, tile_cols, 8, head_count, head_width).transpose(1, 0, 2, 3, 4).reshape(tile_cols, 64, head_count, head_width)
        key_bands = jnp.stack([band_rows[:, 8 * tile_col:8 * tile_col + 14] for tile_col in range(tile_cols)], 0)
        key_bands = key_bands.reshape(tile_cols, 196, 2 * inner_width)
        key_part = key_bands[..., :inner_width].reshape(tile_cols, 196, head_count, head_width)
        value_part = key_bands[..., inner_width:].reshape(tile_cols, 196, head_count, head_width)
        link_row = lax.dynamic_index_in_dim(tile_links, tile_row, 0, keepdims=False).astype(jnp.float32)
        allowed = window[None] * jnp.dot(link_row, pickers)[:, None, :]
        scores = jnp.einsum('cqhd,ckhd->chqk', query_tiles.astype(jnp.float32), key_part.astype(jnp.float32))
        expo = jnp.exp(scores * (scales / head_width)[None, :, None, None]) * allowed[:, None]
        weighting = (expo / lax.optimization_barrier(jnp.sum(expo, axis=-1, keepdims=True))).astype(jnp.bfloat16)
        mixture = jnp.einsum('chqk,ckhd->cqhd', weighting.astype(jnp.float32), value_part.astype(jnp.float32))
        mixture = mixture.astype(jnp.bfloat16)
        return mixture.reshape(tile_cols, 8, 8, inner_width).transpose(1, 0, 2, 3).reshape(8, col_count, inner_width)
    result = lax.map(one_row, jnp.arange(row_count // 8))
    return result.reshape(row_count, col_count, inner_width)

def block(stream, gain_row, weights, scales, tile_links, inner_width):
    row_count, col_count = (stream.shape[0], stream.shape[1])
    normed = (rms_rows(stream) * gain_row).astype(jnp.bfloat16)
    projected = jnp.dot(normed.reshape(row_count * col_count, -1), weights[:3 * inner_width].T, preferred_element_type=jnp.float32)
    projected = projected.reshape(row_count, col_count, 3 * inner_width)
    queries = unit_heads(projected[..., :inner_width], HS).astype(jnp.bfloat16)
    key_part = unit_heads(projected[..., inner_width:2 * inner_width], HS).astype(jnp.bfloat16)
    value_part = projected[..., 2 * inner_width:].astype(jnp.bfloat16)
    mixture = attention(queries, jnp.concatenate([key_part, value_part], axis=-1), tile_links, scales)
    update = jnp.dot(mixture.reshape(row_count * col_count, inner_width), weights[3 * inner_width:4 * inner_width], preferred_element_type=jnp.float32)
    return stream + update.reshape(row_count, col_count, -1)

def reference(clean_frames, noise, noise_steps, noise_freqs, cond_weights, patch_in, patch_out, section_weights, head_scales, fine_links, coarse_links):
    sigmas = jnp.exp(LOG_LOW + noise_steps.astype(jnp.float32) / (STEPS - 1) * (LOG_HIGH - LOG_LOW))
    phases = 2.0 * math.pi * (jnp.log(sigmas) / 4.0)[:, None] * noise_freqs[None, :]
    features = jnp.concatenate([jnp.cos(phases), jnp.sin(phases)], axis=1)
    gains = 1.0 + jnp.einsum('mf,sfd->smd', features, cond_weights.astype(jnp.float32), precision=lax.Precision.HIGHEST)
    fine_inner = H0 * HS
    coarse_inner = H1 * HS
    grid_rows = FR // 4
    grid_cols = FC // 4
    outputs = []
    for micro_batch in range(MB):
        level = sigmas[micro_batch]
        scaled = (clean_frames[micro_batch] + level * noise[micro_batch]) * lax.rsqrt(level * level + 0.25)
        patches = scaled.reshape(grid_rows, 4, grid_cols, 4).transpose(0, 2, 1, 3).reshape(grid_rows * grid_cols, PP)
        embedded = jnp.dot(patches, patch_in, precision=lax.Precision.HIGHEST, preferred_element_type=jnp.float32).reshape(grid_rows, grid_cols, D)
        fine_down = block(embedded, gains[0, micro_batch], section_weights[0], head_scales[0, :H0], fine_links, fine_inner)
        skip_fine = fine_down.astype(jnp.bfloat16)
        grouped = skip_fine.reshape(grid_rows // 2, 2, grid_cols // 2, 2, D).transpose(0, 2, 1, 3, 4).reshape(-1, 4 * D)
        merged = jnp.dot(grouped, section_weights[0, 4 * fine_inner:], preferred_element_type=jnp.float32).astype(jnp.bfloat16)
        merged = merged.reshape(grid_rows // 2, grid_cols // 2, D)
        coarse_down = block(merged.astype(jnp.float32), gains[1, micro_batch], section_weights[1], head_scales[1], coarse_links, coarse_inner).astype(jnp.bfloat16)
        coarse_up = block(coarse_down.astype(jnp.float32), gains[2, micro_batch], section_weights[2], head_scales[2], coarse_links, coarse_inner).astype(jnp.bfloat16)
        widened = jnp.dot(coarse_up.reshape(-1, D), section_weights[3, 4 * fine_inner:].T, preferred_element_type=jnp.float32)
        widened = widened.reshape(grid_rows // 2, grid_cols // 2, 2, 2, D).transpose(0, 2, 1, 3, 4).reshape(grid_rows, grid_cols, D)
        widened = widened + skip_fine.astype(jnp.float32)
        fine_up = block(widened, gains[3, micro_batch], section_weights[3], head_scales[3, :H0], fine_links, fine_inner)
        normed_top = rms_rows(fine_up).astype(jnp.bfloat16)
        pixels = jnp.dot(normed_top.reshape(-1, D), patch_out, preferred_element_type=jnp.float32)
        pixels = pixels.reshape(grid_rows, grid_cols, 4, 4).transpose(0, 2, 1, 3).reshape(grid_rows * 4, grid_cols * 4)
        outputs.append(pixels)
    return jnp.stack(outputs, 0)
```

```python
import functools
import math

import jax
import jax.numpy as jnp
from jax import lax
from jax.experimental import pallas as pl
from jax.experimental.pallas import tpu as pltpu
from jax.sharding import PartitionSpec as P

STEPS = 1000
MB = 2
D = 1024
FI = 512
CI = 1536
G = 256
OWN = 256
FINE = 384
COWN = 64
COARSE = 128
EPS = 1e-06

LOG_LOW = math.log(0.002)
LOG_HIGH = math.log(80.0)
LOG2E = 1.0 / math.log(2.0)

F32 = jnp.float32
BF16 = jnp.bfloat16
NT = (((1,), (1,)), ((), ()))
NN = (((1,), (0,)), ((), ()))

CHUNK = 512
CHUNKS = 12


def dot_nt(a, b):
    return lax.dot_general(a, b, NT, preferred_element_type=F32)


def dot_nn(a, b):
    return lax.dot_general(a, b, NN, preferred_element_type=F32)


def iota(shape, dim):
    return lax.broadcasted_iota(jnp.int32, shape, dim)


def split3(value):
    hi = value.astype(BF16)
    rest = value - hi.astype(F32)
    mid = rest.astype(BF16)
    return hi, mid, (rest - mid.astype(F32)).astype(BF16)


def kernel(
    n_space,
    frames, noise, steps, freqs, cond, patch_in, patch_out, w_hbm, scales, fine_links, coarse_links,
    out,
    w, xs, x, nrm, q_s, k_s, v_s, mix, grp, skip, cin, cout, w3, pox, gains, qscale, links, fmask, cmask, pixout, pixin,
    w_sem, halo_s, halo_r, link_s, link_r, c_s, c_r, skip_s, skip_r, fwd_s, fwd_r, pix_s, pix_r,
):
    s = lax.axis_index("segment")
    p = lax.axis_index("space")
    b = p + (s // 2) * (1 - 2 * (p % 2))
    has_up = b > 0
    has_down = b < n_space - 1

    def place(seg, block):
        return block + (seg // 2) * (1 - 2 * (block % 2))

    def remote(src, dst, ssem, rsem, seg, block):
        return pltpu.make_async_remote_copy(
            src_ref=src, dst_ref=dst, send_sem=ssem, recv_sem=rsem,
            device_id=(seg, place(seg, block)), device_id_type=pl.DeviceIdType.MESH,
        )

    def arrived(dst, rsem):
        pltpu.make_async_remote_copy(
            src_ref=dst, dst_ref=dst, send_sem=rsem, recv_sem=rsem,
            device_id=(s, p), device_id_type=pl.DeviceIdType.MESH,
        ).wait_recv()

    def weight_copy(i):
        return pltpu.make_async_copy(
            w_hbm.at[0, pl.ds(i * CHUNK, CHUNK), :], w.at[pl.ds(i * CHUNK, CHUNK), :], w_sem.at[i]
        )

    barrier = pltpu.get_barrier_semaphore()

    def greet(seg, space):
        pl.semaphore_signal(barrier, inc=1, device_id=(seg, space), device_id_type=pl.DeviceIdType.MESH)

    greet(3, place(3, p))

    @pl.when(s > 0)
    def _():
        greet(s - 1, place(s - 1, b))

        @pl.when(has_up)
        def _():
            greet(s - 1, place(s - 1, b - 1))

        @pl.when(has_down)
        def _():
            greet(s - 1, place(s - 1, b + 1))

    @pl.when((s == 0) | (s == 3))
    def _():
        @pl.when(has_up)
        def _():
            greet(s, place(s, b - 1))

        @pl.when(has_down)
        def _():
            greet(s, place(s, b + 1))

    @pl.when(s == 3)
    def _():
        greet(0, b)

    for i in range(CHUNKS):
        weight_copy(i).start()

    def level_row(m):
        step = jnp.full((1, 128), steps[m], jnp.int32).astype(F32)
        return jnp.exp(LOG_LOW + step / (STEPS - 1) * (LOG_HIGH - LOG_LOW))

    freq_row = freqs[...].reshape(1, 128)
    rows = []
    for m in range(MB):
        phases = 2.0 * math.pi * (jnp.log(level_row(m)) / 4.0) * freq_row
        rows.append(jnp.concatenate([jnp.cos(phases), jnp.sin(phases)], axis=1))
    features = jnp.concatenate(rows + [jnp.zeros((6, 256), F32)], axis=0)
    hi, mid, low = split3(features)
    gains[...] = 1.0 + (dot_nn(hi, cond[0]) + dot_nn(mid, cond[0]) + dot_nn(low, cond[0]))

    lane = iota((1, G), 1) // 64
    for g in range(6):
        four = [scales[0, 4 * g + h] for h in range(4)]
        row = jnp.where(lane == 0, four[0], jnp.where(lane == 1, four[1], jnp.where(lane == 2, four[2], four[3])))
        qscale[g : g + 1, :] = row * (LOG2E / 64.0)

    head_mean = jnp.where(iota((G, G), 0) // 64 == iota((G, G), 1) // 64, 1.0 / 64.0, 0.0).astype(BF16)
    ones = jnp.ones((G, 128), BF16)

    @pl.when(s == 0)
    def _():
        key = iota((1, 256), 1)
        key_row = key // 16
        key_tile = (key % 8) // 4
        for t in range(2):
            for c in range(2):
                row = jnp.zeros((1, 256), F32)
                for dy in range(3):
                    in_row = (key_row >= (0, 4, 12)[dy]) & (key_row < (4, 12, 16)[dy])
                    for kc in range(2):
                        link = fine_links[t, c, 3 * dy + kc - c + 1].astype(F32)
                        row = jnp.where(in_row & (key_tile == kc), link, row)
                links[2 * t + c : 2 * t + c + 1, :] = row

    @pl.when(s == 1)
    def _():
        key_row = iota((1, 256), 1) // 8
        row = jnp.zeros((1, 256), F32)
        for dy in range(3):
            in_row = (key_row >= (0, 4, 12)[dy]) & (key_row < (4, 12, 16)[dy])
            row = jnp.where(in_row, coarse_links[0, 0, 3 * dy + 1].astype(F32), row)
        links[0:1, :] = row

    def make_fine_mask():
        query = iota((128, 256), 0)
        key = iota((128, 256), 1)
        row_gap = key // 16 - 4 - query // 16
        query_col = 2 * (query % 8) + (query // 8) % 2
        key_col = 2 * (key % 8) + (key // 8) % 2
        col_gap = key_col - query_col
        near = (row_gap <= 3) & (row_gap >= -3) & (col_gap <= 3) & (col_gap >= -3)
        for t in range(2):
            left = jnp.broadcast_to(links[2 * t : 2 * t + 1, :], (128, 256))
            right = jnp.broadcast_to(links[2 * t + 1 : 2 * t + 2, :], (128, 256))
            value = jnp.where(query_col < 8, left, right)
            fmask[t] = jnp.where(near, value, 0.0).astype(BF16)

    def make_coarse_mask():
        query = iota((64, 128), 0)
        key = iota((64, 128), 1)
        row_gap = key // 8 - 4 - query // 8
        col_gap = key % 8 - query % 8
        near = (row_gap <= 3) & (row_gap >= -3) & (col_gap <= 3) & (col_gap >= -3)
        value = jnp.broadcast_to(links[0:1, 0:128], (64, 128))
        cmask[...] = jnp.where(near, value, 0.0).astype(BF16)

    @pl.when(s == 0)
    def _():
        for m in range(MB):
            level = level_row(m)[:, 0:64]
            scaled = (frames[m] + level * noise[m]) * lax.rsqrt(level * level + 0.25)
            xs[m, 16:80, :] = jnp.concatenate([scaled, jnp.zeros((64, 64), F32)], axis=1)

        @pl.when(b == 0)
        def _():
            xs[:, 0:16, :] = jnp.zeros((MB, 16, 128), F32)

        @pl.when(b == n_space - 1)
        def _():
            xs[:, 80:96, :] = jnp.zeros((MB, 16, 128), F32)

    @pl.when((s == 1) | (s == 2))
    def _():
        @pl.when(b == 0)
        def _():
            cin[:, 0:32, :] = jnp.zeros((MB, 32, D), BF16)

        @pl.when(b == n_space - 1)
        def _():
            cin[:, 96:128, :] = jnp.zeros((MB, 32, D), BF16)

    @pl.when(s == 3)
    def _():
        @pl.when(b == 0)
        def _():
            cin[:, 16:32, :] = jnp.zeros((MB, 16, D), BF16)
            skip[:, 0:64, :] = jnp.zeros((MB, 64, D), BF16)

        @pl.when(b == n_space - 1)
        def _():
            cin[:, 96:112, :] = jnp.zeros((MB, 16, D), BF16)
            skip[:, 320:384, :] = jnp.zeros((MB, 64, D), BF16)

    edges = has_up.astype(jnp.int32) + has_down.astype(jnp.int32)
    for seg, targets in ((0, 2 + 2 * edges), (1, 1 + edges), (2, 1 + edges), (3, 4 + edges)):

        @pl.when(s == seg)
        def _():
            pl.semaphore_wait(barrier, targets)

    def halo_up():
        return remote(xs.at[:, pl.ds(16, 16), :], xs.at[:, pl.ds(80, 16), :], halo_s.at[0], halo_r.at[1], 0, b - 1)

    def halo_down():
        return remote(xs.at[:, pl.ds(64, 16), :], xs.at[:, pl.ds(0, 16), :], halo_s.at[1], halo_r.at[0], 0, b + 1)

    def link_copy(seg):
        return remote(links, links, link_s, link_r, seg, b)

    @pl.when(s == 0)
    def _():
        @pl.when(has_up)
        def _():
            halo_up().start()

        @pl.when(has_down)
        def _():
            halo_down().start()

        link_copy(3).start()
        make_fine_mask()

        entry = iota((256, 16), 0)
        pick = (iota((256, 16), 1) == 4 * (entry // 64) + entry % 4).astype(BF16)
        hi, low, _ = split3(patch_in[...])
        wide = dot_nn(pick, hi).astype(BF16)
        w3[0:256, :] = wide
        w3[256:512, :] = dot_nn(pick, low).astype(BF16)
        w3[512:768, :] = wide

        @pl.when(has_up)
        def _():
            arrived(xs.at[:, pl.ds(0, 16), :], halo_r.at[0])

        @pl.when(has_down)
        def _():
            arrived(xs.at[:, pl.ds(80, 16), :], halo_r.at[1])

    @pl.when(s == 1)
    def _():
        link_copy(2).start()
        make_coarse_mask()

    @pl.when(s == 2)
    def _():
        arrived(links, link_r)
        make_coarse_mask()

    @pl.when(s == 3)
    def _():
        arrived(links, link_r)
        make_fine_mask()
        entry = iota((16, 256), 0)
        col = iota((16, 256), 1)
        pick = (entry == 4 * ((col // 16) % 4) + col % 4).astype(BF16)
        pox[...] = dot_nn(patch_out[...], pick).astype(BF16)

    @pl.when(s == 0)
    def _():
        for i in range(4):
            weight_copy(i).wait()

    @pl.when(s > 0)
    def _():
        for i in range(CHUNKS):
            weight_copy(i).wait()

    def project(source, rows_q, rows_kv, inner):
        groups = inner // G
        for part, dst in ((0, q_s), (1, k_s), (2, v_s)):
            first, count = rows_q if part == 0 else rows_kv
            for g in range(groups):
                at = part * inner + g * G
                block = dot_nt(source[first : first + count, :], w[at : at + G, :])
                if part < 2:
                    power = dot_nn((block * block).astype(BF16), head_mean)
                    block = block * lax.rsqrt(power + EPS)
                if part == 0:
                    block = block * qscale[g : g + 1, :]
                dst[g, 0:count, :] = block.astype(BF16)

    def attend(queries, keys, values, mask, count):
        head = iota((count, G), 1) // 64
        stacked = jnp.concatenate(
            [jnp.where(head == h, queries, jnp.zeros_like(queries)) for h in range(4)], axis=0
        )
        expo = jnp.exp2(dot_nt(stacked, keys)).astype(BF16)
        expo = expo * jnp.concatenate([mask] * 4, axis=0)
        mixed = dot_nn(expo, values)
        total = dot_nn(expo, ones[0 : keys.shape[0], :])
        part = [mixed[h * count : (h + 1) * count] for h in range(4)]
        sums = [total[h * count : (h + 1) * count] for h in range(4)]
        left = head[:, 0:128] == 0
        right = head[:, 0:128] == 0
        number = jnp.concatenate(
            [
                jnp.where(left, part[0][:, 0:128], part[1][:, 0:128]),
                jnp.where(right, part[2][:, 128:256], part[3][:, 128:256]),
            ],
            axis=1,
        )
        weight = jnp.concatenate(
            [jnp.where(left, sums[0], sums[1]), jnp.where(right, sums[2], sums[3])], axis=1
        )
        return (number / weight).astype(BF16)

    def normed(value, m):
        scale = lax.rsqrt(jnp.mean(value * value, axis=-1, keepdims=True) + EPS)
        return (value * scale * gains[pl.ds(m, 1), :]).astype(BF16)

    def embed(m):
        rows4 = [xs[m, pl.ds(a, 24, stride=4), :] for a in range(4)]
        flat = jnp.concatenate(
            [rows4[0] + pltpu.roll(rows4[1], 64, 1), rows4[2] + pltpu.roll(rows4[3], 64, 1)], axis=1
        )
        hi, low, _ = split3(flat)
        token = iota((16, 256), 0)
        col = iota((16, 256), 1)
        own = ((col % 64) // 4 == 2 * (token % 8) + token // 8).astype(F32)

        def spread(piece):
            wide = jnp.broadcast_to(piece.astype(F32)[:, None, :], (24, 16, 256)) * own[None]
            return wide.reshape(FINE, 256).astype(BF16)

        first = spread(hi)
        lhs = jnp.concatenate([first, first, spread(low)], axis=1)
        x[...] = dot_nn(lhs, w3[...]).reshape(12, 2, 2, 8, D)

    def widen(m):
        coarse = cin[m, 16:112, :]
        for a in range(2):
            for c in range(2):
                at = 4 * FI + (2 * a + c) * D
                x[:, a, c] = dot_nt(coarse, w[at : at + D, :]).reshape(12, 8, D)
        x[...] += skip[m].astype(F32).reshape(12, 2, 2, 8, D)

    def fine_block(m):
        nrm[...] = normed(x[...].reshape(FINE, D), m)
        project(nrm, (64, OWN), (0, FINE), FI)
        for t in range(2):
            for g in range(2):
                mix[128 * t : 128 * t + 128, g * G : (g + 1) * G] = attend(
                    q_s[g, 128 * t : 128 * t + 128, :],
                    k_s[g, 128 * t : 128 * t + 256, :],
                    v_s[g, 128 * t : 128 * t + 256, :],
                    fmask[t],
                    128,
                )
        update = dot_nn(mix[:, 0:FI], w[3 * FI : 4 * FI, :])
        x[2:10] += update.reshape(8, 2, 2, 8, D)

    def coarse_block(m):
        nrm[0:COARSE, :] = normed(cin[m].astype(F32), m)
        project(nrm, (32, COWN), (0, COARSE), CI)
        for g in range(6):
            mix[0:COWN, g * G : (g + 1) * G] = attend(
                q_s[g, 0:COWN, :], k_s[g, 0:COARSE, :], v_s[g, 0:COARSE, :], cmask[...], COWN
            )
        update = dot_nn(mix[0:COWN, :], w[3 * CI : 4 * CI, :])
        cout[m] = (cin[m, 32:96, :].astype(F32) + update).astype(BF16)

    def merge(m):
        own = x[2:10]
        skip[m, 64:320, :] = own.reshape(OWN, D).astype(BF16)
        for a in range(2):
            for c in range(2):
                at = (2 * a + c) * D
                grp[:, at : at + D] = own[:, a, c].reshape(COWN, D).astype(BF16)

        @pl.when(m == 0)
        def _():
            for i in range(4, CHUNKS):
                weight_copy(i).wait()

        cout[m] = dot_nn(grp[...], w[4 * FI :, :]).astype(BF16)

    def head(m):
        top = x[2:10].reshape(OWN, D)
        scale = lax.rsqrt(jnp.mean(top * top, axis=-1, keepdims=True) + EPS)
        pixels = dot_nn((top * scale).astype(BF16), pox[...])
        token = iota((16, 256), 0)
        col = iota((16, 256), 1)
        own = 2 * (token % 8) + token // 8 == 4 * (col // 64) + (col // 4) % 4
        spread = jnp.where(own[None], pixels.reshape(16, 16, 256), 0.0)
        placed = jnp.sum(spread, axis=1)
        pixout[m, 0] = placed[:, 0:128]
        pixout[m, 1] = placed[:, 128:256]

    def coarse_own(m, seg):
        return remote(cout.at[m], cin.at[m, pl.ds(32, 64), :], c_s.at[m, 0], c_r.at[m, 0], seg + 1, b)

    def coarse_up(m, seg, rows):
        return remote(
            cout.at[m, pl.ds(0, rows), :], cin.at[m, pl.ds(96, rows), :], c_s.at[m, 1], c_r.at[m, 2], seg + 1, b - 1
        )

    def coarse_down(m, seg, rows):
        return remote(
            cout.at[m, pl.ds(64 - rows, rows), :], cin.at[m, pl.ds(32 - rows, rows), :],
            c_s.at[m, 2], c_r.at[m, 1], seg + 1, b + 1,
        )

    def send_coarse(m, seg, rows, act):
        @pl.when(has_up)
        def _():
            act(coarse_up(m, seg, rows))

        @pl.when(has_down)
        def _():
            act(coarse_down(m, seg, rows))

        act(coarse_own(m, seg))

    def take_coarse(m, rows):
        arrived(cin.at[m, pl.ds(32, 64), :], c_r.at[m, 0])

        @pl.when(has_up)
        def _():
            arrived(cin.at[m, pl.ds(32 - rows, rows), :], c_r.at[m, 1])

        @pl.when(has_down)
        def _():
            arrived(cin.at[m, pl.ds(96, rows), :], c_r.at[m, 2])

    def skip_copy(m):
        return remote(
            skip.at[m, pl.ds(64, OWN), :], skip.at[m, pl.ds(64, OWN), :], skip_s.at[m], skip_r.at[m], 3, b
        )

    def skip_up(m):
        return remote(
            skip.at[m, pl.ds(64, 64), :], skip.at[m, pl.ds(320, 64), :], fwd_s.at[m, 0], fwd_r.at[m, 1], 3, b - 1
        )

    def skip_down(m):
        return remote(
            skip.at[m, pl.ds(256, 64), :], skip.at[m, pl.ds(0, 64), :], fwd_s.at[m, 1], fwd_r.at[m, 0], 3, b + 1
        )

    def forward_skip(m, act):
        @pl.when(has_up)
        def _():
            act(skip_up(m))

        @pl.when(has_down)
        def _():
            act(skip_down(m))

    def pixel_copy(m, seg):
        return pltpu.make_async_remote_copy(
            src_ref=pixout.at[m, seg // 2], dst_ref=pixin.at[m], send_sem=pix_s.at[m, seg], recv_sem=pix_r.at[m],
            device_id=(seg, b), device_id_type=pl.DeviceIdType.MESH,
        )

    def start(copy):
        copy.start()

    def sent(copy):
        copy.wait_send()

    def one_batch(m, carry):
        @pl.when(s == 0)
        def _():
            embed(m)

        @pl.when(s == 3)
        def _():
            @pl.when(m == 0)
            def _():
                arrived(skip.at[0, pl.ds(64, OWN), :], skip_r.at[0])
                forward_skip(0, start)

            take_coarse(m, 16)

            @pl.when(has_up)
            def _():
                arrived(skip.at[m, pl.ds(0, 64), :], fwd_r.at[m, 0])

            @pl.when(has_down)
            def _():
                arrived(skip.at[m, pl.ds(320, 64), :], fwd_r.at[m, 1])

            widen(m)

            @pl.when(m == 0)
            def _():
                arrived(skip.at[1, pl.ds(64, OWN), :], skip_r.at[1])
                forward_skip(1, start)

        @pl.when((s == 0) | (s == 3))
        def _():
            fine_block(m)

        @pl.when(s == 0)
        def _():
            merge(m)
            send_coarse(m, 0, 32, start)
            skip_copy(m).start()

        @pl.when(s == 3)
        def _():
            head(m)
            for seg in range(4):
                pixel_copy(m, seg).start()

        @pl.when((s == 1) | (s == 2))
        def _():
            take_coarse(m, 32)
            coarse_block(m)

        @pl.when(s == 1)
        def _():
            send_coarse(m, 1, 32, start)

        @pl.when(s == 2)
        def _():
            send_coarse(m, 2, 16, start)

        return carry

    lax.fori_loop(0, MB, one_batch, 0)

    for m in range(MB):
        arrived(pixin.at[m], pix_r.at[m])
        pixels = pixin[m]
        pixels = jnp.where(s % 2 == 1, pltpu.roll(pixels, 64, 1), pixels)
        for a in range(4):
            out[m, pl.ds(a, 16, stride=4), :] = pixels[:, 16 * a : 16 * a + 16]

    @pl.when(s == 0)
    def _():
        @pl.when(has_up)
        def _():
            halo_up().wait_send()

        @pl.when(has_down)
        def _():
            halo_down().wait_send()

        link_copy(3).wait_send()
        for m in range(MB):
            send_coarse(m, 0, 32, sent)
            skip_copy(m).wait_send()

    @pl.when(s == 1)
    def _():
        link_copy(2).wait_send()
        for m in range(MB):
            send_coarse(m, 1, 32, sent)

    @pl.when(s == 2)
    def _():
        for m in range(MB):
            send_coarse(m, 2, 16, sent)

    @pl.when(s == 3)
    def _():
        for m in range(MB):
            forward_skip(m, sent)
            for seg in range(4):
                pixel_copy(m, seg).wait_send()


def per_device(
    clean_frames, noise, noise_steps, noise_freqs, cond_weights, patch_in, patch_out, section_weights, head_scales,
    fine_links, coarse_links,
):
    vmem = pl.BlockSpec(memory_space=pltpu.VMEM)
    smem = pl.BlockSpec(memory_space=pltpu.SMEM)
    hbm = pl.BlockSpec(memory_space=pl.ANY)
    dma = pltpu.SemaphoreType.DMA
    return pl.pallas_call(
        functools.partial(kernel, lax.axis_size("space")),
        out_shape=jax.ShapeDtypeStruct((MB, 64, 16), F32),
        in_specs=[vmem, vmem, smem, vmem, vmem, vmem, vmem, hbm, smem, smem, smem],
        out_specs=vmem,
        scratch_shapes=[
            pltpu.VMEM((6144, D), BF16),
            pltpu.VMEM((MB, 96, 128), F32),
            pltpu.VMEM((12, 2, 2, 8, D), F32),
            pltpu.VMEM((FINE, D), BF16),
            pltpu.VMEM((6, OWN, G), BF16),
            pltpu.VMEM((6, FINE, G), BF16),
            pltpu.VMEM((6, FINE, G), BF16),
            pltpu.VMEM((OWN, CI), BF16),
            pltpu.VMEM((COWN, 4 * D), BF16),
            pltpu.VMEM((MB, FINE, D), BF16),
            pltpu.VMEM((MB, COARSE, D), BF16),
            pltpu.VMEM((MB, COWN, D), BF16),
            pltpu.VMEM((768, D), BF16),
            pltpu.VMEM((D, 256), BF16),
            pltpu.VMEM((8, D), F32),
            pltpu.VMEM((8, G), F32),
            pltpu.VMEM((8, 256), F32),
            pltpu.VMEM((2, 128, 256), BF16),
            pltpu.VMEM((64, 128), BF16),
            pltpu.VMEM((MB, 2, 16, 128), F32),
            pltpu.VMEM((MB, 16, 128), F32),
            dma((CHUNKS,)),
            dma((2,)), dma((2,)),
            dma(()), dma(()),
            dma((MB, 3)), dma((MB, 3)),
            dma((MB,)), dma((MB,)),
            dma((MB, 2)), dma((MB, 2)),
            dma((MB, 4)), dma((MB,)),
        ],
        compiler_params=pltpu.CompilerParams(
            collective_id=0, has_side_effects=True, vmem_limit_bytes=56 << 20
        ),
    )(
        clean_frames, noise, noise_steps, noise_freqs, cond_weights, patch_in, patch_out, section_weights,
        head_scales, fine_links, coarse_links,
    )


def solution(mesh):
    in_specs = (
        P(None, "space", None),
        P(None, "space", None),
        P(),
        P(),
        P("segment", None, None),
        P(),
        P(),
        P("segment", None, None),
        P("segment", None),
        P("space", None, None),
        P("space", None, None),
    )
    out_specs = P(None, "space", "segment")
    return jax.shard_map(
        per_device, mesh=mesh, in_specs=in_specs, out_specs=out_specs, check_vma=False
    )
```

```python
import functools
import math

import jax
import jax.numpy as jnp
from jax import lax
from jax.experimental import pallas as pl
from jax.experimental.pallas import tpu as pltpu
from jax.sharding import PartitionSpec as P

STEPS = 1000
MB = 2
D = 1024
FI = 512
CI = 1536
G = 256
OWN = 256
FINE = 384
COWN = 64
COARSE = 128
EPS = 1e-06

LOG_LOW = math.log(0.002)
LOG_HIGH = math.log(80.0)
LOG2E = 1.0 / math.log(2.0)

F32 = jnp.float32
BF16 = jnp.bfloat16
NT = (((1,), (1,)), ((), ()))
NN = (((1,), (0,)), ((), ()))

CHUNK = 256
CHUNKS = 24


def dot_nt(a, b):
    return lax.dot_general(a, b, NT, preferred_element_type=F32)


def dot_nn(a, b):
    return lax.dot_general(a, b, NN, preferred_element_type=F32)


def iota(shape, dim):
    return lax.broadcasted_iota(jnp.int32, shape, dim)


def split3(value):
    hi = value.astype(BF16)
    rest = value - hi.astype(F32)
    mid = rest.astype(BF16)
    return hi, mid, (rest - mid.astype(F32)).astype(BF16)


def kernel(
    n_space,
    frames_hbm, noise_hbm, steps, freqs_hbm, cond_hbm, patch_in_hbm, patch_out_hbm, w_hbm, scales, fine_links,
    coarse_links,
    out,
    w, wt, frames, noise, freqs, cond, patch_in, patch_out, xs, x, nrm, halo, q_s, k_s, v_s, mix, grp, skip, cin, cout,
    w3, pox, gains, qscale, links, fmask, cmask, pixout, pixin, placed,
    w_sem, in_sem, halo_s, halo_r, link_s, link_r, c_s, c_r, skip_s, skip_r, fwd_s, fwd_r, pix_s, pix_r,
):
    s = lax.axis_index("segment")
    p = lax.axis_index("space")
    b = p + (s // 2) * (1 - 2 * (p % 2))
    has_up = b > 0
    has_down = b < n_space - 1

    def place(seg, block):
        return block + (seg // 2) * (1 - 2 * (block % 2))

    def remote(src, dst, ssem, rsem, seg, block):
        return pltpu.make_async_remote_copy(
            src_ref=src, dst_ref=dst, send_sem=ssem, recv_sem=rsem,
            device_id=(seg, place(seg, block)), device_id_type=pl.DeviceIdType.MESH,
        )

    def arrived(dst, rsem):
        pltpu.make_async_remote_copy(
            src_ref=dst, dst_ref=dst, send_sem=rsem, recv_sem=rsem,
            device_id=(s, p), device_id_type=pl.DeviceIdType.MESH,
        ).wait_recv()

    def weight_copy(i):
        rows = pl.ds(i * CHUNK, CHUNK)
        return pltpu.make_async_copy(w_hbm.at[0, rows, :], w.at[rows, :], w_sem.at[i])

    freq_copy = pltpu.make_async_copy(freqs_hbm, freqs, in_sem.at[0])
    cond_copy = pltpu.make_async_copy(cond_hbm, cond, in_sem.at[1])
    frame_copy = pltpu.make_async_copy(frames_hbm, frames, in_sem.at[2])
    noise_copy = pltpu.make_async_copy(noise_hbm, noise, in_sem.at[3])
    patch_in_copy = pltpu.make_async_copy(patch_in_hbm, patch_in, in_sem.at[4])
    patch_out_copy = pltpu.make_async_copy(patch_out_hbm, patch_out, in_sem.at[5])

    barrier = pltpu.get_barrier_semaphore()

    def greet(seg, space):
        pl.semaphore_signal(barrier, inc=1, device_id=(seg, space), device_id_type=pl.DeviceIdType.MESH)

    @pl.when((s == 0) | (s == 3))
    def _():
        @pl.when(has_up)
        def _():
            greet(s, place(s, b - 1))

        @pl.when(has_down)
        def _():
            greet(s, place(s, b + 1))

    @pl.when(s == 0)
    def _():
        frame_copy.start()
        noise_copy.start()
        patch_in_copy.start()

    freq_copy.start()
    cond_copy.start()
    for i in range(CHUNKS):
        weight_copy(i).start()

    greet(3, place(3, p))

    @pl.when(s > 0)
    def _():
        greet(s - 1, place(s - 1, b))

        @pl.when(has_up)
        def _():
            greet(s - 1, place(s - 1, b - 1))

        @pl.when(has_down)
        def _():
            greet(s - 1, place(s - 1, b + 1))

    @pl.when(s == 3)
    def _():
        greet(0, b)
        patch_out_copy.start()

    def level_row(m):
        step = jnp.full((1, 128), steps[m], jnp.int32).astype(F32)
        return jnp.exp(LOG_LOW + step / (STEPS - 1) * (LOG_HIGH - LOG_LOW))

    lane = iota((1, G), 1) // 64
    for g in range(6):
        four = [scales[0, 4 * g + h] for h in range(4)]
        row = jnp.where(lane == 0, four[0], jnp.where(lane == 1, four[1], jnp.where(lane == 2, four[2], four[3])))
        qscale[g : g + 1, :] = row * (LOG2E / 64.0)

    head_mean = jnp.where(iota((G, G), 0) // 64 == iota((G, G), 1) // 64, 1.0 / 64.0, 0.0).astype(BF16)
    ones = jnp.ones((G, 128), BF16)

    def make_gains():
        rows = []
        for m in range(MB):
            phases = 2.0 * math.pi * (jnp.log(level_row(m)) / 4.0) * freqs[...].reshape(1, 128)
            rows.append(jnp.concatenate([jnp.cos(phases), jnp.sin(phases)], axis=1))
        features = jnp.concatenate(rows + [jnp.zeros((6, 256), F32)], axis=0)
        hi, mid, low = split3(features)
        gains[...] = 1.0 + (dot_nn(hi, cond[0]) + dot_nn(mid, cond[0]) + dot_nn(low, cond[0]))

    def make_fine_mask():
        query = iota((128, 256), 0)
        key = iota((128, 256), 1)
        row_gap = key // 16 - 4 - query // 16
        query_col = 2 * (query % 8) + (query // 8) % 2
        key_col = 2 * (key % 8) + (key // 8) % 2
        col_gap = key_col - query_col
        near = (row_gap <= 3) & (row_gap >= -3) & (col_gap <= 3) & (col_gap >= -3)
        for t in range(2):
            left = jnp.broadcast_to(links[2 * t : 2 * t + 1, :], (128, 256))
            right = jnp.broadcast_to(links[2 * t + 1 : 2 * t + 2, :], (128, 256))
            value = jnp.where(query_col < 8, left, right)
            fmask[t] = jnp.where(near, value, 0.0).astype(BF16)

    def make_coarse_mask():
        query = iota((64, 128), 0)
        key = iota((64, 128), 1)
        row_gap = key // 8 - 4 - query // 8
        col_gap = key % 8 - query % 8
        near = (row_gap <= 3) & (row_gap >= -3) & (col_gap <= 3) & (col_gap >= -3)
        value = jnp.broadcast_to(links[0:1, 0:128], (64, 128))
        cmask[...] = jnp.where(near, value, 0.0).astype(BF16)

    def make_fine_links():
        key = iota((1, 256), 1)
        key_row = key // 16
        key_tile = (key % 8) // 4
        for t in range(2):
            for c in range(2):
                row = jnp.zeros((1, 256), F32)
                for dy in range(3):
                    in_row = (key_row >= (0, 4, 12)[dy]) & (key_row < (4, 12, 16)[dy])
                    for kc in range(2):
                        link = fine_links[t, c, 3 * dy + kc - c + 1].astype(F32)
                        row = jnp.where(in_row & (key_tile == kc), link, row)
                links[2 * t + c : 2 * t + c + 1, :] = row

    def make_coarse_links():
        key_row = iota((1, 256), 1) // 8
        row = jnp.zeros((1, 256), F32)
        for dy in range(3):
            in_row = (key_row >= (0, 4, 12)[dy]) & (key_row < (4, 12, 16)[dy])
            row = jnp.where(in_row, coarse_links[0, 0, 3 * dy + 1].astype(F32), row)
        links[0:1, :] = row

    def halo_up():
        return remote(xs.at[:, pl.ds(16, 16), :], xs.at[:, pl.ds(80, 16), :], halo_s.at[0], halo_r.at[1], 0, b - 1)

    def halo_down():
        return remote(xs.at[:, pl.ds(64, 16), :], xs.at[:, pl.ds(0, 16), :], halo_s.at[1], halo_r.at[0], 0, b + 1)

    def link_copy(seg):
        return remote(links, links, link_s, link_r, seg, b)

    edges = has_up.astype(jnp.int32) + has_down.astype(jnp.int32)

    def scale_pixels():
        for m in range(MB):
            level = level_row(m)[:, 0:64]
            scaled = (frames[m] + level * noise[m]) * lax.rsqrt(level * level + 0.25)
            xs[m, 16:80, :] = jnp.concatenate([scaled, jnp.zeros((64, 64), F32)], axis=1)

        @pl.when(b == 0)
        def _():
            xs[:, 0:16, :] = jnp.zeros((MB, 16, 128), F32)

        @pl.when(b == n_space - 1)
        def _():
            xs[:, 80:96, :] = jnp.zeros((MB, 16, 128), F32)

    def make_embedding():
        entry = iota((256, 16), 0)
        pick = (iota((256, 16), 1) == 4 * (entry // 64) + entry % 4).astype(BF16)
        hi, low, _ = split3(patch_in[...])
        wide = dot_nn(pick, hi).astype(BF16)
        w3[0:256, :] = wide
        w3[256:512, :] = dot_nn(pick, low).astype(BF16)
        w3[512:768, :] = wide

    def transpose_weights(first, count):
        eye = (iota((G, G), 0) == iota((G, G), 1)).astype(BF16)

        def tile(i, carry):
            weight_copy(first + i).wait()
            row = pl.multiple_of((first + i) * G, G)
            col = pl.multiple_of(i * G, G)
            for k in range(D // G):
                block = dot_nt(eye, w[pl.ds(row, G), k * G : (k + 1) * G])
                wt[k * G : (k + 1) * G, pl.ds(col, G)] = block.astype(BF16)
            return carry

        lax.fori_loop(0, count, tile, 0)

    def normed(value, m):
        scale = lax.rsqrt(jnp.mean(value * value, axis=-1, keepdims=True) + EPS)
        return (value * scale * gains[pl.ds(m, 1), :]).astype(BF16)

    def embed(rows4):
        flat = jnp.concatenate(
            [rows4[0] + pltpu.roll(rows4[1], 64, 1), rows4[2] + pltpu.roll(rows4[3], 64, 1)], axis=1
        )
        hi, low, _ = split3(flat)
        token = iota((16, 256), 0)
        col = iota((16, 256), 1)
        own = ((col % 64) // 4 == 2 * (token % 8) + token // 8).astype(F32)
        count = flat.shape[0]

        def spread(piece):
            wide = jnp.broadcast_to(piece.astype(F32)[:, None, :], (count, 16, 256)) * own[None]
            return wide.reshape(count * 16, 256).astype(BF16)

        first = spread(hi)
        return dot_nn(jnp.concatenate([first, first, spread(low)], axis=1), w3[...])

    def run_jobs(jobs):
        def finish(block, part, g, put):
            if part < 2:
                power = dot_nn((block * block).astype(BF16), head_mean)
                block = block * lax.rsqrt(power + EPS)
            if part == 0:
                block = block * qscale[g : g + 1, :]
            put(block.astype(BF16))

        pending = []
        for make, part, g, put in jobs:
            pending.append((make(), part, g, put))
            if len(pending) > 2:
                finish(*pending.pop(0))
        for job in pending:
            finish(*job)

    def fine_jobs(source, first, count, parts, put):
        jobs = []
        for part in parts:
            for g in range(FI // G):
                at = part * FI + g * G
                lo, n = (first, count) if part == 0 else (0, source.shape[0])
                jobs.append(
                    (
                        lambda at=at, lo=lo, n=n: dot_nt(source[lo : lo + n, :], w[at : at + G, :]),
                        part, g, functools.partial(put, part, g),
                    )
                )
        return jobs

    def embed_own():
        for m in range(MB):
            own = embed([xs[m, pl.ds(16 + a, 16, stride=4), :] for a in range(4)])
            x[m, 2:10] = own.reshape(8, 2, 2, 8, D)
            nrm[m * OWN : (m + 1) * OWN, :] = normed(own, m)

    def project_own():
        def put(part, g, block):
            for m in range(MB):
                rows = block[m * OWN : (m + 1) * OWN]
                if part == 0:
                    q_s[2 * m + g, :, :] = rows
                else:
                    (k_s if part == 1 else v_s)[2 * m + g, 64:320, :] = rows

        run_jobs(fine_jobs(nrm, 0, 2 * OWN, (0, 1, 2), put))

    def project_halo():
        for m in range(MB):
            rows4 = [
                jnp.concatenate(
                    [xs[m, pl.ds(a, 4, stride=4), :], xs[m, pl.ds(80 + a, 4, stride=4), :]], axis=0
                )
                for a in range(4)
            ]
            halo[m * 128 : (m + 1) * 128, :] = normed(embed(rows4), m)

        def put(part, g, block):
            dst = k_s if part == 1 else v_s
            for m in range(MB):
                dst[2 * m + g, 0:64, :] = block[m * 128 : m * 128 + 64]
                dst[2 * m + g, 320:384, :] = block[m * 128 + 64 : m * 128 + 128]

        run_jobs(fine_jobs(halo, 0, 256, (1, 2), put))

    def widen(m):
        coarse = cin[m, 16:112, :]
        for a in range(2):
            for c in range(2):
                at = (2 * a + c) * D
                x[m, :, a, c] = dot_nn(coarse, wt[:, at : at + D]).reshape(12, 8, D)
        x[m] += skip[m].astype(F32).reshape(12, 2, 2, 8, D)

    def project_fine(m):
        nrm[0:FINE, :] = normed(x[m].reshape(FINE, D), m)

        def put(part, g, block):
            (q_s, k_s, v_s)[part][2 * m + g, :, :] = block

        run_jobs(fine_jobs(nrm.at[0:FINE], 64, OWN, (0, 1, 2), put))

    def attend(queries, keys, values, mask, count):
        head = iota((count, G), 1) // 64
        stacked = jnp.concatenate(
            [jnp.where(head == h, queries, jnp.zeros_like(queries)) for h in range(4)], axis=0
        )
        expo = jnp.exp2(dot_nt(stacked, keys)).astype(BF16)
        expo = expo * jnp.concatenate([mask] * 4, axis=0)
        mixed = dot_nn(expo, values)
        total = dot_nn(expo, ones[0 : keys.shape[0], :])
        part = [mixed[h * count : (h + 1) * count] for h in range(4)]
        sums = [total[h * count : (h + 1) * count] for h in range(4)]
        first = head[:, 0:128] == 0
        number = jnp.concatenate(
            [
                jnp.where(first, part[0][:, 0:128], part[1][:, 0:128]),
                jnp.where(first, part[2][:, 128:256], part[3][:, 128:256]),
            ],
            axis=1,
        )
        weight = jnp.concatenate(
            [jnp.where(first, sums[0], sums[1]), jnp.where(first, sums[2], sums[3])], axis=1
        )
        return (number / weight).astype(BF16)

    def mix_fine(m):
        for t in range(2):
            for g in range(2):
                mix[128 * t : 128 * t + 128, g * G : (g + 1) * G] = attend(
                    q_s[2 * m + g, 128 * t : 128 * t + 128, :],
                    k_s[2 * m + g, 128 * t : 128 * t + 256, :],
                    v_s[2 * m + g, 128 * t : 128 * t + 256, :],
                    fmask[t],
                    128,
                )
        update = dot_nn(mix[:, 0:FI], w[3 * FI : 4 * FI, :])
        x[m, 2:10] += update.reshape(8, 2, 2, 8, D)

    def coarse_jobs(first, count, parts):
        jobs = []
        for part in parts:
            for g in range(CI // G):
                at = part * CI + g * G

                def put(block, part=part, g=g):
                    (q_s, k_s, v_s)[part][g, 0:count, :] = block

                jobs.append(
                    (lambda at=at: dot_nn(nrm[first : first + count, :], wt[:, at : at + G]), part, g, put)
                )
        return jobs

    def coarse_queries(m):
        nrm[32:96, :] = normed(cin[m, 32:96, :].astype(F32), m)
        run_jobs(coarse_jobs(32, COWN, (0,)))

    def coarse_rest(m):
        nrm[0:32, :] = normed(cin[m, 0:32, :].astype(F32), m)
        nrm[96:128, :] = normed(cin[m, 96:128, :].astype(F32), m)
        run_jobs(coarse_jobs(0, COARSE, (1, 2)))
        for g in range(6):
            mix[0:COWN, g * G : (g + 1) * G] = attend(
                q_s[g, 0:COWN, :], k_s[g, 0:COARSE, :], v_s[g, 0:COARSE, :], cmask[...], COWN
            )
        update = dot_nn(mix[0:COWN, :], w[3 * CI : 4 * CI, :])
        cout[m] = (cin[m, 32:96, :].astype(F32) + update).astype(BF16)

    def merge(m):
        own = x[m, 2:10]
        skip[m, 64:320, :] = own.reshape(OWN, D).astype(BF16)
        for a in range(2):
            for c in range(2):
                at = (2 * a + c) * D
                grp[:, at : at + D] = own[:, a, c].reshape(COWN, D).astype(BF16)
        cout[m] = dot_nn(grp[...], w[4 * FI :, :]).astype(BF16)

    def head(m):
        top = x[m, 2:10].reshape(OWN, D)
        scale = lax.rsqrt(jnp.mean(top * top, axis=-1, keepdims=True) + EPS)
        pixels = dot_nn((top * scale).astype(BF16), pox[...])
        token = iota((16, 256), 0)
        col = iota((16, 256), 1)
        own = 2 * (token % 8) + token // 8 == 4 * (col // 64) + (col // 4) % 4
        spread = jnp.where(own[None], pixels.reshape(16, 16, 256), 0.0)
        total = jnp.sum(spread, axis=1)
        pixout[m, 0] = total[:, 0:128]
        pixout[m, 1] = total[:, 128:256]

    def coarse_own(m, seg):
        return remote(cout.at[m], cin.at[m, pl.ds(32, 64), :], c_s.at[m, 0], c_r.at[m, 0], seg + 1, b)

    def coarse_up(m, seg, rows):
        return remote(
            cout.at[m, pl.ds(0, rows), :], cin.at[m, pl.ds(96, rows), :], c_s.at[m, 1], c_r.at[m, 2], seg + 1, b - 1
        )

    def coarse_down(m, seg, rows):
        return remote(
            cout.at[m, pl.ds(64 - rows, rows), :], cin.at[m, pl.ds(32 - rows, rows), :],
            c_s.at[m, 2], c_r.at[m, 1], seg + 1, b + 1,
        )

    def send_coarse(m, seg, rows, act):
        @pl.when(has_up)
        def _():
            act(coarse_up(m, seg, rows))

        @pl.when(has_down)
        def _():
            act(coarse_down(m, seg, rows))

        act(coarse_own(m, seg))

    def take_own(m):
        arrived(cin.at[m, pl.ds(32, 64), :], c_r.at[m, 0])

    def take_halos(m, rows):
        @pl.when(has_up)
        def _():
            arrived(cin.at[m, pl.ds(32 - rows, rows), :], c_r.at[m, 1])

        @pl.when(has_down)
        def _():
            arrived(cin.at[m, pl.ds(96, rows), :], c_r.at[m, 2])

    def skip_copy(m):
        return remote(
            skip.at[m, pl.ds(64, OWN), :], skip.at[m, pl.ds(64, OWN), :], skip_s.at[m], skip_r.at[m], 3, b
        )

    def skip_up(m):
        return remote(
            skip.at[m, pl.ds(64, 64), :], skip.at[m, pl.ds(320, 64), :], fwd_s.at[m, 0], fwd_r.at[m, 1], 3, b - 1
        )

    def skip_down(m):
        return remote(
            skip.at[m, pl.ds(256, 64), :], skip.at[m, pl.ds(0, 64), :], fwd_s.at[m, 1], fwd_r.at[m, 0], 3, b + 1
        )

    def forward_skip(m, act):
        @pl.when(has_up)
        def _():
            act(skip_up(m))

        @pl.when(has_down)
        def _():
            act(skip_down(m))

    def pixel_copy(m, seg):
        return pltpu.make_async_remote_copy(
            src_ref=pixout.at[m, seg // 2], dst_ref=pixin.at[m], send_sem=pix_s.at[m, seg], recv_sem=pix_r.at[m],
            device_id=(seg, b), device_id_type=pl.DeviceIdType.MESH,
        )

    def start(copy):
        copy.start()

    def sent(copy):
        copy.wait_send()

    freq_copy.wait()
    cond_copy.wait()
    make_gains()

    @pl.when(s == 0)
    def _():
        frame_copy.wait()
        noise_copy.wait()
        scale_pixels()
        patch_in_copy.wait()
        make_embedding()
        make_fine_links()
        make_fine_mask()
        embed_own()
        pl.semaphore_wait(barrier, 2 + 2 * edges)

        @pl.when(has_up)
        def _():
            halo_up().start()

        @pl.when(has_down)
        def _():
            halo_down().start()

        link_copy(3).start()
        for i in range(3 * FI // CHUNK):
            weight_copy(i).wait()
        project_own()

        @pl.when(has_up)
        def _():
            arrived(xs.at[:, pl.ds(0, 16), :], halo_r.at[0])

        @pl.when(has_down)
        def _():
            arrived(xs.at[:, pl.ds(80, 16), :], halo_r.at[1])

        project_halo()
        for i in range(3 * FI // CHUNK, CHUNKS):
            weight_copy(i).wait()

    @pl.when((s == 1) | (s == 2))
    def _():
        @pl.when(b == 0)
        def _():
            cin[:, 0:32, :] = jnp.zeros((MB, 32, D), BF16)

        @pl.when(b == n_space - 1)
        def _():
            cin[:, 96:128, :] = jnp.zeros((MB, 32, D), BF16)

        transpose_weights(0, 3 * CI // G)
        for i in range(3 * CI // CHUNK, CHUNKS):
            weight_copy(i).wait()
        pl.semaphore_wait(barrier, 1 + edges)

    @pl.when(s == 1)
    def _():
        make_coarse_links()
        link_copy(2).start()
        make_coarse_mask()

    @pl.when(s == 2)
    def _():
        arrived(links, link_r)
        make_coarse_mask()

    @pl.when(s == 3)
    def _():
        @pl.when(b == 0)
        def _():
            cin[:, 16:32, :] = jnp.zeros((MB, 16, D), BF16)
            skip[:, 0:64, :] = jnp.zeros((MB, 64, D), BF16)

        @pl.when(b == n_space - 1)
        def _():
            cin[:, 96:112, :] = jnp.zeros((MB, 16, D), BF16)
            skip[:, 320:384, :] = jnp.zeros((MB, 64, D), BF16)

        for i in range(4 * FI // CHUNK):
            weight_copy(i).wait()
        transpose_weights(4 * FI // G, 4 * D // G)
        patch_out_copy.wait()
        entry = iota((16, 256), 0)
        col = iota((16, 256), 1)
        pick = (entry == 4 * ((col // 16) % 4) + col % 4).astype(BF16)
        pox[...] = lax.dot_general(
            patch_out[...], pick, (((0,), (0,)), ((), ())), preferred_element_type=F32
        ).astype(BF16)
        pl.semaphore_wait(barrier, 4 + edges)
        arrived(links, link_r)
        make_fine_mask()
        arrived(skip.at[0, pl.ds(64, OWN), :], skip_r.at[0])
        forward_skip(0, start)

    def one_batch(m, carry):
        @pl.when(s == 3)
        def _():
            take_own(m)
            take_halos(m, 16)

            @pl.when(has_up)
            def _():
                arrived(skip.at[m, pl.ds(0, 64), :], fwd_r.at[m, 0])

            @pl.when(has_down)
            def _():
                arrived(skip.at[m, pl.ds(320, 64), :], fwd_r.at[m, 1])

            widen(m)

            @pl.when(m == 0)
            def _():
                arrived(skip.at[1, pl.ds(64, OWN), :], skip_r.at[1])
                forward_skip(1, start)

            project_fine(m)

        @pl.when((s == 0) | (s == 3))
        def _():
            mix_fine(m)

        @pl.when(s == 0)
        def _():
            merge(m)
            send_coarse(m, 0, 32, start)
            skip_copy(m).start()

        @pl.when(s == 3)
        def _():
            head(m)
            for seg in range(4):
                pixel_copy(m, seg).start()

        @pl.when((s == 1) | (s == 2))
        def _():
            take_own(m)
            coarse_queries(m)
            take_halos(m, 32)
            coarse_rest(m)

        @pl.when(s == 1)
        def _():
            send_coarse(m, 1, 32, start)

        @pl.when(s == 2)
        def _():
            send_coarse(m, 2, 16, start)

        return carry

    lax.fori_loop(0, MB, one_batch, 0)

    for m in range(MB):
        arrived(pixin.at[m], pix_r.at[m])
        pixels = pixin[m]
        pixels = jnp.where(s % 2 == 1, pltpu.roll(pixels, 64, 1), pixels)
        for a in range(4):
            placed[pl.ds(a, 16, stride=4), :] = pltpu.roll(pixels, (128 - 16 * a) % 128, 1)
        out[m] = placed[...].T[0:16, :]

    @pl.when(s == 0)
    def _():
        @pl.when(has_up)
        def _():
            halo_up().wait_send()

        @pl.when(has_down)
        def _():
            halo_down().wait_send()

        link_copy(3).wait_send()
        for m in range(MB):
            send_coarse(m, 0, 32, sent)
            skip_copy(m).wait_send()

    @pl.when(s == 1)
    def _():
        link_copy(2).wait_send()
        for m in range(MB):
            send_coarse(m, 1, 32, sent)

    @pl.when(s == 2)
    def _():
        for m in range(MB):
            send_coarse(m, 2, 16, sent)

    @pl.when(s == 3)
    def _():
        for m in range(MB):
            forward_skip(m, sent)
            for seg in range(4):
                pixel_copy(m, seg).wait_send()


def per_device(
    clean_frames, noise, noise_steps, noise_freqs, cond_weights, patch_in, patch_out, section_weights, head_scales,
    fine_links, coarse_links,
):
    vmem = pl.BlockSpec(memory_space=pltpu.VMEM)
    smem = pl.BlockSpec(memory_space=pltpu.SMEM)
    hbm = pl.BlockSpec(memory_space=pl.ANY)
    dma = pltpu.SemaphoreType.DMA
    placed = pl.pallas_call(
        functools.partial(kernel, lax.axis_size("space")),
        out_shape=jax.ShapeDtypeStruct((MB, 16, 64), F32),
        in_specs=[hbm, hbm, smem, hbm, hbm, hbm, hbm, hbm, smem, smem, smem],
        out_specs=vmem,
        scratch_shapes=[
            pltpu.VMEM((6144, D), BF16),
            pltpu.VMEM((D, 3 * CI), BF16),
            pltpu.VMEM((MB, 64, 64), F32),
            pltpu.VMEM((MB, 64, 64), F32),
            pltpu.VMEM((128,), F32),
            pltpu.VMEM((1, 256, D), BF16),
            pltpu.VMEM((16, D), F32),
            pltpu.VMEM((16, D), BF16),
            pltpu.VMEM((MB, 96, 128), F32),
            pltpu.VMEM((MB, 12, 2, 2, 8, D), F32),
            pltpu.VMEM((2 * OWN, D), BF16),
            pltpu.VMEM((256, D), BF16),
            pltpu.VMEM((6, OWN, G), BF16),
            pltpu.VMEM((6, FINE, G), BF16),
            pltpu.VMEM((6, FINE, G), BF16),
            pltpu.VMEM((OWN, CI), BF16),
            pltpu.VMEM((COWN, 4 * D), BF16),
            pltpu.VMEM((MB, FINE, D), BF16),
            pltpu.VMEM((MB, COARSE, D), BF16),
            pltpu.VMEM((MB, COWN, D), BF16),
            pltpu.VMEM((768, D), BF16),
            pltpu.VMEM((D, 256), BF16),
            pltpu.VMEM((8, D), F32),
            pltpu.VMEM((8, G), F32),
            pltpu.VMEM((8, 256), F32),
            pltpu.VMEM((2, 128, 256), BF16),
            pltpu.VMEM((64, 128), BF16),
            pltpu.VMEM((MB, 2, 16, 128), F32),
            pltpu.VMEM((MB, 16, 128), F32),
            pltpu.VMEM((64, 128), F32),
            dma((CHUNKS,)),
            dma((6,)),
            dma((2,)), dma((2,)),
            dma(()), dma(()),
            dma((MB, 3)), dma((MB, 3)),
            dma((MB,)), dma((MB,)),
            dma((MB, 2)), dma((MB, 2)),
            dma((MB, 4)), dma((MB,)),
        ],
        compiler_params=pltpu.CompilerParams(
            collective_id=0, has_side_effects=True, vmem_limit_bytes=58 << 20
        ),
    )(
        clean_frames, noise, noise_steps, noise_freqs, cond_weights, patch_in, patch_out.T, section_weights,
        head_scales, fine_links, coarse_links,
    )
    return placed.transpose(0, 2, 1)


def solution(mesh):
    in_specs = (
        P(None, "space", None),
        P(None, "space", None),
        P(),
        P(),
        P("segment", None, None),
        P(),
        P(),
        P("segment", None, None),
        P("segment", None),
        P("space", None, None),
        P("space", None, None),
    )
    out_specs = P(None, "space", "segment")
    return jax.shard_map(
        per_device, mesh=mesh, in_specs=in_specs, out_specs=out_specs, check_vma=False
    )
```

```python
import functools
import math

import jax
import jax.numpy as jnp
from jax import lax
from jax.experimental import pallas as pl
from jax.experimental.pallas import tpu as pltpu
from jax.sharding import PartitionSpec as P

STEPS = 1000
MB = 2
D = 1024
FI = 512
CI = 1536
G = 256
OWN = 256
FINE = 384
COWN = 64
COARSE = 128
EPS = 1e-06

LOG_LOW = math.log(0.002)
LOG_HIGH = math.log(80.0)
LOG2E = 1.0 / math.log(2.0)

F32 = jnp.float32
BF16 = jnp.bfloat16
NT = (((1,), (1,)), ((), ()))
NN = (((1,), (0,)), ((), ()))

CHUNK = 256
CHUNKS = 24


def dot_nt(a, b):
    return lax.dot_general(a, b, NT, preferred_element_type=F32)


def dot_nn(a, b):
    return lax.dot_general(a, b, NN, preferred_element_type=F32)


def iota(shape, dim):
    return lax.broadcasted_iota(jnp.int32, shape, dim)


def split3(value):
    hi = value.astype(BF16)
    rest = value - hi.astype(F32)
    mid = rest.astype(BF16)
    return hi, mid, (rest - mid.astype(F32)).astype(BF16)


def kernel(
    n_space,
    frames_hbm, noise_hbm, steps, freqs_hbm, cond_hbm, patch_in_hbm, patch_out_hbm, w_hbm, scales, fine_links,
    coarse_links,
    out,
    w, wt, frames, noise, freqs, cond, patch_in, patch_out, xs, x, nrm, halo, q_s, k_s, v_s, mix, mixed, grp, wo, cin, cout,
    edge_out, edge_in, w3, pox, gains, qscale, links, fmask, cmask, pixout, pixin, placed,
    w_sem, in_sem, halo_s, halo_r, link_s, link_r, c_s, c_r, xs_s, xs_r, wo_s, wo_r, mix_s, mix_r, fwd_s,
    fwd_r, pix_s, pix_r,
):
    s = lax.axis_index("segment")
    p = lax.axis_index("space")
    b = p + (s // 2) * (1 - 2 * (p % 2))
    has_up = b > 0
    has_down = b < n_space - 1

    def place(seg, block):
        return block + (seg // 2) * (1 - 2 * (block % 2))

    def remote(src, dst, ssem, rsem, seg, block):
        return pltpu.make_async_remote_copy(
            src_ref=src, dst_ref=dst, send_sem=ssem, recv_sem=rsem,
            device_id=(seg, place(seg, block)), device_id_type=pl.DeviceIdType.MESH,
        )

    def arrived(dst, rsem):
        pltpu.make_async_remote_copy(
            src_ref=dst, dst_ref=dst, send_sem=rsem, recv_sem=rsem,
            device_id=(s, p), device_id_type=pl.DeviceIdType.MESH,
        ).wait_recv()

    def weight_copy(i):
        rows = pl.ds(i * CHUNK, CHUNK)
        return pltpu.make_async_copy(w_hbm.at[0, rows, :], w.at[rows, :], w_sem.at[i])

    freq_copy = pltpu.make_async_copy(freqs_hbm, freqs, in_sem.at[0])
    cond_copy = pltpu.make_async_copy(cond_hbm, cond, in_sem.at[1])
    frame_copy = pltpu.make_async_copy(frames_hbm, frames, in_sem.at[2])
    noise_copy = pltpu.make_async_copy(noise_hbm, noise, in_sem.at[3])
    patch_in_copy = pltpu.make_async_copy(patch_in_hbm, patch_in, in_sem.at[4])
    patch_out_copy = pltpu.make_async_copy(patch_out_hbm, patch_out, in_sem.at[5])

    barrier = pltpu.get_barrier_semaphore()

    def greet(seg, space):
        pl.semaphore_signal(barrier, inc=1, device_id=(seg, space), device_id_type=pl.DeviceIdType.MESH)

    @pl.when((s == 0) | (s == 3))
    def _():
        @pl.when(has_up)
        def _():
            greet(s, place(s, b - 1))

        @pl.when(has_down)
        def _():
            greet(s, place(s, b + 1))

    @pl.when(s == 0)
    def _():
        frame_copy.start()
        noise_copy.start()

    @pl.when((s == 0) | (s == 3))
    def _():
        patch_in_copy.start()

    freq_copy.start()
    cond_copy.start()
    for i in range(CHUNKS):
        weight_copy(i).start()

    greet(3, place(3, p))

    @pl.when(s > 0)
    def _():
        greet(s - 1, place(s - 1, b))

        @pl.when(has_up)
        def _():
            greet(s - 1, place(s - 1, b - 1))

        @pl.when(has_down)
        def _():
            greet(s - 1, place(s - 1, b + 1))

    @pl.when(s == 3)
    def _():
        greet(0, b)
        patch_out_copy.start()

    def level_row(m):
        step = jnp.full((1, 128), steps[m], jnp.int32).astype(F32)
        return jnp.exp(LOG_LOW + step / (STEPS - 1) * (LOG_HIGH - LOG_LOW))

    lane = iota((1, G), 1) // 64
    for g in range(6):
        four = [scales[0, 4 * g + h] for h in range(4)]
        row = jnp.where(lane == 0, four[0], jnp.where(lane == 1, four[1], jnp.where(lane == 2, four[2], four[3])))
        qscale[g : g + 1, :] = row * (LOG2E / 64.0)

    head_mean = jnp.where(iota((G, G), 0) // 64 == iota((G, G), 1) // 64, 1.0 / 64.0, 0.0).astype(BF16)

    def make_gains():
        rows = []
        for m in range(MB):
            phases = 2.0 * math.pi * (jnp.log(level_row(m)) / 4.0) * freqs[...].reshape(1, 128)
            rows.append(jnp.concatenate([jnp.cos(phases), jnp.sin(phases)], axis=1))
        features = jnp.concatenate(rows + [jnp.zeros((6, 256), F32)], axis=0)
        hi, mid, low = split3(features)
        gains[...] = 1.0 + (dot_nn(hi, cond[0]) + dot_nn(mid, cond[0]) + dot_nn(low, cond[0]))

    def make_fine_mask():
        query = iota((128, 256), 0)
        key = iota((128, 256), 1)
        row_gap = key // 16 - 4 - query // 16
        query_col = 2 * (query % 8) + (query // 8) % 2
        key_col = 2 * (key % 8) + (key // 8) % 2
        col_gap = key_col - query_col
        near = (row_gap <= 3) & (row_gap >= -3) & (col_gap <= 3) & (col_gap >= -3)
        for t in range(2):
            left = jnp.broadcast_to(links[2 * t : 2 * t + 1, :], (128, 256))
            right = jnp.broadcast_to(links[2 * t + 1 : 2 * t + 2, :], (128, 256))
            value = jnp.where(query_col < 8, left, right)
            fmask[t] = jnp.where(near, value, 0.0).astype(BF16)

    def make_coarse_mask():
        query = iota((64, 128), 0)
        key = iota((64, 128), 1)
        row_gap = key // 8 - 4 - query // 8
        col_gap = key % 8 - query % 8
        near = (row_gap <= 3) & (row_gap >= -3) & (col_gap <= 3) & (col_gap >= -3)
        value = jnp.broadcast_to(links[0:1, 0:128], (64, 128))
        cmask[...] = jnp.where(near, value, 0.0).astype(BF16)

    def make_fine_links():
        key = iota((1, 256), 1)
        key_row = key // 16
        key_tile = (key % 8) // 4
        for t in range(2):
            for c in range(2):
                row = jnp.zeros((1, 256), F32)
                for dy in range(3):
                    in_row = (key_row >= (0, 4, 12)[dy]) & (key_row < (4, 12, 16)[dy])
                    for kc in range(2):
                        link = fine_links[t, c, 3 * dy + kc - c + 1].astype(F32)
                        row = jnp.where(in_row & (key_tile == kc), link, row)
                links[2 * t + c : 2 * t + c + 1, :] = row

    def make_coarse_links():
        key_row = iota((1, 256), 1) // 8
        row = jnp.zeros((1, 256), F32)
        for dy in range(3):
            in_row = (key_row >= (0, 4, 12)[dy]) & (key_row < (4, 12, 16)[dy])
            row = jnp.where(in_row, coarse_links[0, 0, 3 * dy + 1].astype(F32), row)
        links[0:1, :] = row

    def halo_up():
        return remote(xs.at[:, pl.ds(16, 16), :], xs.at[:, pl.ds(80, 16), :], halo_s.at[0], halo_r.at[1], 0, b - 1)

    def halo_down():
        return remote(xs.at[:, pl.ds(64, 16), :], xs.at[:, pl.ds(0, 16), :], halo_s.at[1], halo_r.at[0], 0, b + 1)

    def link_copy(seg):
        return remote(links, links, link_s, link_r, seg, b)

    edges = has_up.astype(jnp.int32) + has_down.astype(jnp.int32)

    def scale_pixels():
        for m in range(MB):
            level = level_row(m)[:, 0:64]
            scaled = (frames[m] + level * noise[m]) * lax.rsqrt(level * level + 0.25)
            xs[m, 16:80, :] = jnp.concatenate([scaled, jnp.zeros((64, 64), F32)], axis=1)

        @pl.when(b == 0)
        def _():
            xs[:, 0:16, :] = jnp.zeros((MB, 16, 128), F32)

        @pl.when(b == n_space - 1)
        def _():
            xs[:, 80:96, :] = jnp.zeros((MB, 16, 128), F32)

    def make_embedding():
        entry = iota((256, 16), 0)
        pick = (iota((256, 16), 1) == 4 * (entry // 64) + entry % 4).astype(BF16)
        hi, low, _ = split3(patch_in[...])
        wide = dot_nn(pick, hi).astype(BF16)
        w3[0:256, :] = wide
        w3[256:512, :] = dot_nn(pick, low).astype(BF16)
        w3[512:768, :] = wide

    def transpose_weights(first, count):
        eye = (iota((G, G), 0) == iota((G, G), 1)).astype(BF16)

        def tile(i, carry):
            weight_copy(first + i).wait()
            row = pl.multiple_of((first + i) * G, G)
            col = pl.multiple_of(i * G, G)
            for k in range(D // G):
                block = dot_nt(eye, w[pl.ds(row, G), k * G : (k + 1) * G])
                wt[k * G : (k + 1) * G, pl.ds(col, G)] = block.astype(BF16)
            return carry

        lax.fori_loop(0, count, tile, 0)

    def normed(value, m):
        scale = lax.rsqrt(jnp.mean(value * value, axis=-1, keepdims=True) + EPS)
        return (value * scale * gains[pl.ds(m, 1), :]).astype(BF16)

    def embed(rows4):
        flat = jnp.concatenate(
            [rows4[0] + pltpu.roll(rows4[1], 64, 1), rows4[2] + pltpu.roll(rows4[3], 64, 1)], axis=1
        )
        hi, low, _ = split3(flat)
        token = iota((16, 256), 0)
        col = iota((16, 256), 1)
        own = ((col % 64) // 4 == 2 * (token % 8) + token // 8).astype(F32)
        count = flat.shape[0]

        def spread(piece):
            wide = jnp.broadcast_to(piece.astype(F32)[:, None, :], (count, 16, 256)) * own[None]
            return wide.reshape(count * 16, 256).astype(BF16)

        first = spread(hi)
        return dot_nn(jnp.concatenate([first, first, spread(low)], axis=1), w3[...])

    def run_jobs(jobs):
        def finish(block, part, g, put):
            if part < 2:
                power = dot_nn((block * block).astype(BF16), head_mean)
                block = block * lax.rsqrt(power + EPS)
            if part == 0:
                block = block * qscale[g : g + 1, :]
            put(block.astype(BF16))

        pending = []
        for make, part, g, put in jobs:
            pending.append((make(), part, g, put))
            if len(pending) > 2:
                finish(*pending.pop(0))
        for job in pending:
            finish(*job)

    def fine_jobs(source, first, count, parts, put):
        jobs = []
        for part in parts:
            for g in range(FI // G):
                at = part * FI + g * G
                lo, n = (first, count) if part == 0 else (0, source.shape[0])
                jobs.append(
                    (
                        lambda at=at, lo=lo, n=n: dot_nt(source[lo : lo + n, :], w[at : at + G, :]),
                        part, g, functools.partial(put, part, g),
                    )
                )
        return jobs

    def embed_own(m):
        own = embed([xs[m, pl.ds(16 + a, 16, stride=4), :] for a in range(4)])
        x[m, 2:10] = own.reshape(8, 2, 2, 8, D)
        nrm[m * OWN : (m + 1) * OWN, :] = normed(own, m)

    def project_own(m):
        def put(part, g, block):
            if part == 0:
                q_s[2 * m + g, :, :] = block
            else:
                (k_s if part == 1 else v_s)[2 * m + g, 64:320, :] = block

        own = nrm.at[pl.ds(pl.multiple_of(m * OWN, OWN), OWN), :]
        run_jobs(fine_jobs(own, 0, OWN, (0, 1, 2), put))

    def project_halo(m):
        rows4 = [
            jnp.concatenate([xs[m, pl.ds(a, 4, stride=4), :], xs[m, pl.ds(80 + a, 4, stride=4), :]], axis=0)
            for a in range(4)
        ]
        halo[...] = normed(embed(rows4), m)

        def put(part, g, block):
            dst = k_s if part == 1 else v_s
            dst[2 * m + g, 0:64, :] = block[0:64]
            dst[2 * m + g, 320:384, :] = block[64:128]

        run_jobs(fine_jobs(halo, 0, 128, (1, 2), put))

    def widen(m):
        coarse = cin[m, 16:112, :]
        for a in range(2):
            for c in range(2):
                at = (2 * a + c) * D
                x[m, :, a, c] += dot_nn(coarse, wt[:, at : at + D]).reshape(12, 8, D)

    def embed_all(m):
        embedded = embed([xs[m, pl.ds(a, 24, stride=4), :] for a in range(4)])
        x[m] = embedded.reshape(12, 2, 2, 8, D)

    def make_skip(m):
        whole = (x[m].reshape(FINE, D) + dot_nn(mixed[m], wo[...])).astype(BF16)
        x[m] = whole.astype(F32).reshape(12, 2, 2, 8, D)

    def project_fine(m):
        nrm[0:FINE, :] = normed(x[m].reshape(FINE, D), m)

        def put(part, g, block):
            (q_s, k_s, v_s)[part][2 * m + g, :, :] = block

        run_jobs(fine_jobs(nrm.at[0:FINE], 64, OWN, (0, 1, 2), put))

    def attend(items, lags):
        held = [{} for _ in items]

        def score(i):
            queries, keys = items[i][0](), items[i][1]()
            head = iota(queries.shape, 1) // 64
            stacked = jnp.concatenate(
                [jnp.where(head == h, queries, jnp.zeros_like(queries)) for h in range(4)], axis=0
            )
            held[i]["score"] = dot_nt(stacked, keys)

        def weigh(i):
            expo = jnp.exp2(held[i].pop("score")).astype(BF16)
            held[i]["expo"] = expo * jnp.concatenate([items[i][3]()] * 4, axis=0)

        def gather(i):
            expo = held[i].pop("expo")
            held[i]["sum"] = jnp.sum(expo.astype(F32), axis=-1, keepdims=True)
            held[i]["mixed"] = dot_nn(expo, items[i][2]())

        def place_heads(i):
            total, value = held[i].pop("sum"), held[i].pop("mixed")
            count = value.shape[0] // 4
            part = [value[h * count : (h + 1) * count] for h in range(4)]
            sums = [total[h * count : (h + 1) * count] for h in range(4)]
            first = iota((count, 128), 1) < 64
            number = jnp.concatenate(
                [
                    jnp.where(first, part[0][:, 0:128], part[1][:, 0:128]),
                    jnp.where(first, part[2][:, 128:256], part[3][:, 128:256]),
                ],
                axis=1,
            )
            weight = jnp.concatenate(
                [jnp.where(first, sums[0], sums[1]), jnp.where(first, sums[2], sums[3])], axis=1
            )
            items[i][4]((number / weight).astype(BF16))

        stages = (score, weigh, gather, place_heads)
        for step in range(len(items) + lags[-1]):
            for stage, lag in zip(stages, lags):
                if 0 <= step - lag < len(items):
                    stage(step - lag)

    def mix_fine(m):
        items = []
        for t in range(2):
            for g in range(2):
                rows, near, cols = pl.ds(128 * t, 128), pl.ds(128 * t, 256), pl.ds(g * G, G)

                def put(value, rows=rows, cols=cols):
                    mix[m, rows, cols] = value

                items.append(
                    (
                        lambda g=g, rows=rows: q_s[2 * m + g, rows, :],
                        lambda g=g, near=near: k_s[2 * m + g, near, :],
                        lambda g=g, near=near: v_s[2 * m + g, near, :],
                        lambda t=t: fmask[t],
                        put,
                    )
                )
        attend(items, (0, 1, 1, 2))

    def add_fine(m):
        update = dot_nn(mix[m], w[3 * FI : 4 * FI, :])
        x[m, 2:10] += update.reshape(8, 2, 2, 8, D)

    def coarse_jobs(first, count, parts):
        jobs = []
        for part in parts:
            for g in range(CI // G):
                at = part * CI + g * G

                def put(block, part=part, g=g):
                    (q_s, k_s, v_s)[part][g, 0:count, :] = block

                jobs.append(
                    (lambda at=at: dot_nn(nrm[first : first + count, :], wt[:, at : at + G]), part, g, put)
                )
        return jobs

    def coarse_queries(m):
        nrm[32:96, :] = normed(cin[m, 32:96, :].astype(F32), m)
        run_jobs(coarse_jobs(32, COWN, (0,)))

    def coarse_rest(m):
        for i in range(2):
            edge = edge_in[m, i].astype(F32)
            edge = jnp.concatenate([edge[0:24], edge[24:48]], axis=1)
            at = (8, 96)[i]
            nrm[at : at + 24, :] = normed(edge, m)
        run_jobs(coarse_jobs(0, COARSE, (1, 2)))
        items = []
        for g in range(6):

            def put(value, g=g):
                grp[:, g * G : (g + 1) * G] = value

            items.append(
                (
                    lambda g=g: q_s[g, 0:COWN, :],
                    lambda g=g: k_s[g, 0:COARSE, :],
                    lambda g=g: v_s[g, 0:COARSE, :],
                    lambda: cmask[...],
                    put,
                )
            )
        attend(items, (0, 1, 2, 3))
        update = dot_nn(grp[:, 0:CI], w[3 * CI : 4 * CI, :])
        put_coarse(m, cin[m, 32:96, :].astype(F32) + update)

    def put_coarse(m, result):
        cout[m] = result.astype(BF16)
        for i in range(2):
            rows = result[0:24] if i == 0 else result[40:64]
            edge_out[m, i] = jnp.concatenate([rows[:, 0:512], rows[:, 512:1024]], axis=0).astype(BF16)

    def merge(m):
        own = x[m, 2:10]
        for a in range(2):
            for c in range(2):
                at = (2 * a + c) * D
                grp[:, at : at + D] = own[:, a, c].reshape(COWN, D).astype(BF16)
        put_coarse(m, dot_nn(grp[...], w[4 * FI :, :]))

    def head(m):
        top = x[m, 2:10].reshape(OWN, D)
        scale = lax.rsqrt(jnp.mean(top * top, axis=-1, keepdims=True) + EPS)
        pixels = dot_nn((top * scale).astype(BF16), pox[...])
        token = iota((16, 256), 0)
        col = iota((16, 256), 1)
        own = 2 * (token % 8) + token // 8 == 4 * (col // 64) + (col // 4) % 4
        spread = jnp.where(own[None], pixels.reshape(16, 16, 256), 0.0)
        total = jnp.sum(spread, axis=1)
        pixout[m, 0] = total[:, 0:128]
        pixout[m, 1] = total[:, 128:256]

    def coarse_own(m, seg):
        return remote(cout.at[m], cin.at[m, pl.ds(32, 64), :], c_s.at[m, 0], c_r.at[m, 0], seg + 1, b)

    def edge_up(m, seg):
        if seg < 2:
            src, dst = edge_out.at[m, 0], edge_in.at[m, 1]
        else:
            src, dst = cout.at[m, pl.ds(0, 16), :], cin.at[m, pl.ds(96, 16), :]
        return remote(src, dst, c_s.at[m, 1], c_r.at[m, 2], seg + 1, b - 1)

    def edge_down(m, seg):
        if seg < 2:
            src, dst = edge_out.at[m, 1], edge_in.at[m, 0]
        else:
            src, dst = cout.at[m, pl.ds(48, 16), :], cin.at[m, pl.ds(16, 16), :]
        return remote(src, dst, c_s.at[m, 2], c_r.at[m, 1], seg + 1, b + 1)

    def send_coarse(m, seg, act):
        @pl.when(has_up)
        def _():
            act(edge_up(m, seg))

        @pl.when(has_down)
        def _():
            act(edge_down(m, seg))

        act(coarse_own(m, seg))

    def take_own(m):
        arrived(cin.at[m, pl.ds(32, 64), :], c_r.at[m, 0])

    def take_edges(m, above, below):
        @pl.when(has_up)
        def _():
            arrived(above, c_r.at[m, 1])

        @pl.when(has_down)
        def _():
            arrived(below, c_r.at[m, 2])

    def pixels_on():
        return remote(xs, xs, xs_s, xs_r, 3, b)

    def weights_on():
        return remote(w_hbm.at[0, pl.ds(3 * FI, FI), :], wo, wo_s, wo_r, 3, b)

    def mix_copy(m):
        return remote(mix.at[m], mixed.at[m, pl.ds(64, OWN), :], mix_s.at[m], mix_r.at[m], 3, b)

    def mix_up(m):
        return remote(
            mixed.at[m, pl.ds(64, 64), :], mixed.at[m, pl.ds(320, 64), :], fwd_s.at[m, 0], fwd_r.at[m, 1], 3, b - 1
        )

    def mix_down(m):
        return remote(
            mixed.at[m, pl.ds(256, 64), :], mixed.at[m, pl.ds(0, 64), :], fwd_s.at[m, 1], fwd_r.at[m, 0], 3, b + 1
        )

    def forward_mix(m, act):
        @pl.when(has_up)
        def _():
            act(mix_up(m))

        @pl.when(has_down)
        def _():
            act(mix_down(m))

    def pixel_copy(m, seg):
        return pltpu.make_async_remote_copy(
            src_ref=pixout.at[m, seg // 2], dst_ref=pixin.at[m], send_sem=pix_s.at[m, seg], recv_sem=pix_r.at[m],
            device_id=(seg, b), device_id_type=pl.DeviceIdType.MESH,
        )

    def start(copy):
        copy.start()

    def sent(copy):
        copy.wait_send()

    @pl.when(s == 0)
    def _():
        frame_copy.wait()
        noise_copy.wait()
        scale_pixels()
        pl.semaphore_wait(barrier, 2 + 2 * edges)

        @pl.when(has_up)
        def _():
            halo_up().start()

        @pl.when(has_down)
        def _():
            halo_down().start()

        weights_on().start()

    freq_copy.wait()
    cond_copy.wait()
    make_gains()

    @pl.when((s == 0) | (s == 3))
    def _():
        patch_in_copy.wait()
        make_embedding()

    @pl.when(s == 0)
    def _():
        make_fine_links()
        make_fine_mask()
        link_copy(3).start()
        embed_own(0)
        for i in range(3 * FI // CHUNK):
            weight_copy(i).wait()

    @pl.when((s == 1) | (s == 2))
    def _():
        nrm[0:8, :] = jnp.zeros((8, D), BF16)
        nrm[120:128, :] = jnp.zeros((8, D), BF16)

        @pl.when(b == 0)
        def _():
            edge_in[:, 0] = jnp.zeros((MB, 48, 512), BF16)

        @pl.when(b == n_space - 1)
        def _():
            edge_in[:, 1] = jnp.zeros((MB, 48, 512), BF16)

        transpose_weights(0, 3 * CI // G)
        for i in range(3 * CI // CHUNK, CHUNKS):
            weight_copy(i).wait()
        pl.semaphore_wait(barrier, 1 + edges)

    @pl.when(s == 1)
    def _():
        make_coarse_links()
        link_copy(2).start()
        make_coarse_mask()

    @pl.when(s == 2)
    def _():
        arrived(links, link_r)
        make_coarse_mask()

    @pl.when(s == 3)
    def _():
        @pl.when(b == 0)
        def _():
            cin[:, 16:32, :] = jnp.zeros((MB, 16, D), BF16)
            mixed[:, 0:64, :] = jnp.zeros((MB, 64, FI), BF16)

        @pl.when(b == n_space - 1)
        def _():
            cin[:, 96:112, :] = jnp.zeros((MB, 16, D), BF16)
            mixed[:, 320:384, :] = jnp.zeros((MB, 64, FI), BF16)

        for i in range(4 * FI // CHUNK):
            weight_copy(i).wait()
        transpose_weights(4 * FI // G, 4 * D // G)
        patch_out_copy.wait()
        entry = iota((16, 256), 0)
        col = iota((16, 256), 1)
        pick = (entry == 4 * ((col // 16) % 4) + col % 4).astype(BF16)
        pox[...] = lax.dot_general(
            patch_out[...], pick, (((0,), (0,)), ((), ())), preferred_element_type=F32
        ).astype(BF16)
        pl.semaphore_wait(barrier, 4 + edges)
        arrived(links, link_r)
        make_fine_mask()
        arrived(xs, xs_r)
        for m in range(MB):
            embed_all(m)
        arrived(wo, wo_r)
        for m in range(MB):
            arrived(mixed.at[m, pl.ds(64, OWN), :], mix_r.at[m])
            forward_mix(m, start)
        for m in range(MB):

            @pl.when(has_up)
            def _():
                arrived(mixed.at[m, pl.ds(0, 64), :], fwd_r.at[m, 0])

            @pl.when(has_down)
            def _():
                arrived(mixed.at[m, pl.ds(320, 64), :], fwd_r.at[m, 1])

            make_skip(m)

    def one_batch(m, carry):
        @pl.when(s == 0)
        def _():
            project_own(m)

            @pl.when(m == 0)
            def _():
                embed_own(1)

                @pl.when(has_up)
                def _():
                    arrived(xs.at[:, pl.ds(0, 16), :], halo_r.at[0])

                @pl.when(has_down)
                def _():
                    arrived(xs.at[:, pl.ds(80, 16), :], halo_r.at[1])

                pixels_on().start()
                for i in range(3 * FI // CHUNK, CHUNKS):
                    weight_copy(i).wait()

            project_halo(m)

        @pl.when(s == 3)
        def _():
            take_own(m)
            take_edges(m, cin.at[m, pl.ds(16, 16), :], cin.at[m, pl.ds(96, 16), :])
            widen(m)
            project_fine(m)

        @pl.when((s == 0) | (s == 3))
        def _():
            mix_fine(m)

            @pl.when(s == 0)
            def _():
                mix_copy(m).start()

            add_fine(m)

        @pl.when(s == 0)
        def _():
            merge(m)
            send_coarse(m, 0, start)

        @pl.when(s == 3)
        def _():
            head(m)
            for seg in range(4):
                pixel_copy(m, seg).start()

        @pl.when((s == 1) | (s == 2))
        def _():
            take_own(m)
            coarse_queries(m)
            take_edges(m, edge_in.at[m, 0], edge_in.at[m, 1])
            coarse_rest(m)

        @pl.when(s == 1)
        def _():
            send_coarse(m, 1, start)

        @pl.when(s == 2)
        def _():
            send_coarse(m, 2, start)

        return carry

    lax.fori_loop(0, MB, one_batch, 0)

    for m in range(MB):
        arrived(pixin.at[m], pix_r.at[m])
        pixels = pixin[m]
        pixels = jnp.where(s % 2 == 1, pltpu.roll(pixels, 64, 1), pixels)
        for a in range(4):
            placed[pl.ds(a, 16, stride=4), :] = pltpu.roll(pixels, (128 - 16 * a) % 128, 1)
        out[m] = placed[...].T[0:16, :]

    @pl.when(s == 0)
    def _():
        @pl.when(has_up)
        def _():
            halo_up().wait_send()

        @pl.when(has_down)
        def _():
            halo_down().wait_send()

        link_copy(3).wait_send()
        for m in range(MB):
            send_coarse(m, 0, sent)
            mix_copy(m).wait_send()
        weights_on().wait_send()
        pixels_on().wait_send()

    @pl.when(s == 1)
    def _():
        link_copy(2).wait_send()
        for m in range(MB):
            send_coarse(m, 1, sent)

    @pl.when(s == 2)
    def _():
        for m in range(MB):
            send_coarse(m, 2, sent)

    @pl.when(s == 3)
    def _():
        for m in range(MB):
            forward_mix(m, sent)
            for seg in range(4):
                pixel_copy(m, seg).wait_send()


def per_device(
    clean_frames, noise, noise_steps, noise_freqs, cond_weights, patch_in, patch_out, section_weights, head_scales,
    fine_links, coarse_links,
):
    vmem = pl.BlockSpec(memory_space=pltpu.VMEM)
    smem = pl.BlockSpec(memory_space=pltpu.SMEM)
    hbm = pl.BlockSpec(memory_space=pl.ANY)
    dma = pltpu.SemaphoreType.DMA
    placed = pl.pallas_call(
        functools.partial(kernel, lax.axis_size("space")),
        out_shape=jax.ShapeDtypeStruct((MB, 16, 64), F32),
        in_specs=[hbm, hbm, smem, hbm, hbm, hbm, hbm, hbm, smem, smem, smem],
        out_specs=vmem,
        scratch_shapes=[
            pltpu.VMEM((6144, D), BF16),
            pltpu.VMEM((D, 3 * CI), BF16),
            pltpu.VMEM((MB, 64, 64), F32),
            pltpu.VMEM((MB, 64, 64), F32),
            pltpu.VMEM((128,), F32),
            pltpu.VMEM((1, 256, D), BF16),
            pltpu.VMEM((16, D), F32),
            pltpu.VMEM((16, D), BF16),
            pltpu.VMEM((MB, 96, 128), F32),
            pltpu.VMEM((MB, 12, 2, 2, 8, D), F32),
            pltpu.VMEM((2 * OWN, D), BF16),
            pltpu.VMEM((128, D), BF16),
            pltpu.VMEM((6, OWN, G), BF16),
            pltpu.VMEM((6, FINE, G), BF16),
            pltpu.VMEM((6, FINE, G), BF16),
            pltpu.VMEM((MB, OWN, FI), BF16),
            pltpu.VMEM((MB, FINE, FI), BF16),
            pltpu.VMEM((COWN, 4 * D), BF16),
            pltpu.VMEM((FI, D), BF16),
            pltpu.VMEM((MB, COARSE, D), BF16),
            pltpu.VMEM((MB, COWN, D), BF16),
            pltpu.VMEM((MB, 2, 48, 512), BF16),
            pltpu.VMEM((MB, 2, 48, 512), BF16),
            pltpu.VMEM((768, D), BF16),
            pltpu.VMEM((D, 256), BF16),
            pltpu.VMEM((8, D), F32),
            pltpu.VMEM((8, G), F32),
            pltpu.VMEM((8, 256), F32),
            pltpu.VMEM((2, 128, 256), BF16),
            pltpu.VMEM((64, 128), BF16),
            pltpu.VMEM((MB, 2, 16, 128), F32),
            pltpu.VMEM((MB, 16, 128), F32),
            pltpu.VMEM((64, 128), F32),
            dma((CHUNKS,)),
            dma((6,)),
            dma((2,)), dma((2,)),
            dma(()), dma(()),
            dma((MB, 3)), dma((MB, 3)),
            dma(()), dma(()),
            dma(()), dma(()),
            dma((MB,)), dma((MB,)),
            dma((MB, 2)), dma((MB, 2)),
            dma((MB, 4)), dma((MB,)),
        ],
        compiler_params=pltpu.CompilerParams(
            collective_id=0, has_side_effects=True, vmem_limit_bytes=58 << 20
        ),
    )(
        clean_frames, noise, noise_steps, noise_freqs, cond_weights, patch_in, patch_out.T, section_weights,
        head_scales, fine_links, coarse_links,
    )
    return placed.transpose(0, 2, 1)


def solution(mesh):
    in_specs = (
        P(None, "space", None),
        P(None, "space", None),
        P(),
        P(),
        P("segment", None, None),
        P(),
        P(),
        P("segment", None, None),
        P("segment", None),
        P("space", None, None),
        P("space", None, None),
    )
    out_specs = P(None, "space", "segment")
    return jax.shard_map(
        per_device, mesh=mesh, in_specs=in_specs, out_specs=out_specs, check_vma=False
    )
```

```python
import functools
import math

import jax
import jax.numpy as jnp
from jax import lax
from jax.experimental import pallas as pl
from jax.experimental.pallas import tpu as pltpu
from jax.sharding import PartitionSpec as P

STEPS = 1000
MB = 2
D = 1024
FI = 512
CI = 1536
G = 256
OWN = 256
FINE = 384
COWN = 64
COARSE = 128
EPS = 1e-06

LOG_LOW = math.log(0.002)
LOG_HIGH = math.log(80.0)
LOG2E = 1.0 / math.log(2.0)

F32 = jnp.float32
BF16 = jnp.bfloat16
NT = (((1,), (1,)), ((), ()))
NN = (((1,), (0,)), ((), ()))

CHUNK = 1536
CHUNKS = 4


def dot_nt(a, b):
    return lax.dot_general(a, b, NT, preferred_element_type=F32)


def dot_nn(a, b):
    return lax.dot_general(a, b, NN, preferred_element_type=F32)


def iota(shape, dim):
    return lax.broadcasted_iota(jnp.int32, shape, dim)


def split3(value):
    hi = value.astype(BF16)
    rest = value - hi.astype(F32)
    mid = rest.astype(BF16)
    return hi, mid, (rest - mid.astype(F32)).astype(BF16)


def kernel(
    n_space,
    frames_hbm, noise_hbm, steps, freqs_hbm, cond_hbm, patch_in_hbm, patch_out_hbm, w_hbm, scales, fine_links,
    coarse_links,
    out,
    w, wt, frames, noise, freqs, cond, patch_in, patch_out, xs, x, nrm, halo, q_s, k_s, v_s, mix, mixed, grp, wo, cin, cout,
    edge_out, edge_in, w3, pox, gains, qscale, links, fmask, cmask, pixout, pixin, placed,
    w_sem, in_sem, halo_s, halo_r, link_s, link_r, c_s, c_r, xs_s, xs_r, wo_s, wo_r, wx_s, wx_r, mix_s, mix_r, fwd_s,
    fwd_r, pix_s, pix_r,
):
    s = lax.axis_index("segment")
    p = lax.axis_index("space")
    b = p + (s // 2) * (1 - 2 * (p % 2))
    has_up = b > 0
    has_down = b < n_space - 1

    def place(seg, block):
        return block + (seg // 2) * (1 - 2 * (block % 2))

    def remote(src, dst, ssem, rsem, seg, block):
        return pltpu.make_async_remote_copy(
            src_ref=src, dst_ref=dst, send_sem=ssem, recv_sem=rsem,
            device_id=(seg, place(seg, block)), device_id_type=pl.DeviceIdType.MESH,
        )

    def arrived(dst, rsem):
        pltpu.make_async_remote_copy(
            src_ref=dst, dst_ref=dst, send_sem=rsem, recv_sem=rsem,
            device_id=(s, p), device_id_type=pl.DeviceIdType.MESH,
        ).wait_recv()

    def weight_copy(i):
        rows = pl.ds(i * CHUNK, CHUNK)
        return pltpu.make_async_copy(w_hbm.at[0, rows, :], w.at[rows, :], w_sem.at[i])

    freq_copy = pltpu.make_async_copy(freqs_hbm, freqs, in_sem.at[0])
    cond_copy = pltpu.make_async_copy(cond_hbm, cond, in_sem.at[1])
    frame_copy = pltpu.make_async_copy(frames_hbm, frames, in_sem.at[2])
    noise_copy = pltpu.make_async_copy(noise_hbm, noise, in_sem.at[3])
    patch_in_copy = pltpu.make_async_copy(patch_in_hbm, patch_in, in_sem.at[4])
    patch_out_copy = pltpu.make_async_copy(patch_out_hbm, patch_out, in_sem.at[5])

    barrier = pltpu.get_barrier_semaphore()

    def greet(seg, space):
        pl.semaphore_signal(barrier, inc=1, device_id=(seg, space), device_id_type=pl.DeviceIdType.MESH)

    @pl.when((s == 0) | (s == 3))
    def _():
        @pl.when(has_up)
        def _():
            greet(s, place(s, b - 1))

        @pl.when(has_down)
        def _():
            greet(s, place(s, b + 1))

    @pl.when(s == 0)
    def _():
        frame_copy.start()
        noise_copy.start()

    @pl.when((s == 0) | (s == 3))
    def _():
        patch_in_copy.start()

    freq_copy.start()
    cond_copy.start()
    weight_copy(0).start()

    @pl.when(s > 0)
    def _():
        for i in range(1, CHUNKS):
            weight_copy(i).start()

    greet(3, place(3, p))

    @pl.when(s > 0)
    def _():
        greet(s - 1, place(s - 1, b))

        @pl.when(has_up)
        def _():
            greet(s - 1, place(s - 1, b - 1))

        @pl.when(has_down)
        def _():
            greet(s - 1, place(s - 1, b + 1))

    @pl.when(s == 3)
    def _():
        greet(0, b)
        greet(1, b)
        patch_out_copy.start()

    def level_row(m):
        step = jnp.full((1, 128), steps[m], jnp.int32).astype(F32)
        return jnp.exp(LOG_LOW + step / (STEPS - 1) * (LOG_HIGH - LOG_LOW))

    lane = iota((1, G), 1) // 64
    for g in range(6):
        four = [scales[0, 4 * g + h] for h in range(4)]
        row = jnp.where(lane == 0, four[0], jnp.where(lane == 1, four[1], jnp.where(lane == 2, four[2], four[3])))
        qscale[g : g + 1, :] = row * (LOG2E / 64.0)

    head_mean = jnp.where(iota((G, G), 0) // 64 == iota((G, G), 1) // 64, 1.0 / 64.0, 0.0).astype(BF16)

    def make_gains():
        rows = []
        for m in range(MB):
            phases = 2.0 * math.pi * (jnp.log(level_row(m)) / 4.0) * freqs[...].reshape(1, 128)
            rows.append(jnp.concatenate([jnp.cos(phases), jnp.sin(phases)], axis=1))
        features = jnp.concatenate(rows + [jnp.zeros((6, 256), F32)], axis=0)
        hi, mid, low = split3(features)
        gains[...] = 1.0 + (dot_nn(hi, cond[0]) + dot_nn(mid, cond[0]) + dot_nn(low, cond[0]))

    def make_fine_mask():
        query = iota((128, 256), 0)
        key = iota((128, 256), 1)
        row_gap = key // 16 - 4 - query // 16
        query_col = 2 * (query % 8) + (query // 8) % 2
        key_col = 2 * (key % 8) + (key // 8) % 2
        col_gap = key_col - query_col
        near = (row_gap <= 3) & (row_gap >= -3) & (col_gap <= 3) & (col_gap >= -3)
        for t in range(2):
            left = jnp.broadcast_to(links[2 * t : 2 * t + 1, :], (128, 256))
            right = jnp.broadcast_to(links[2 * t + 1 : 2 * t + 2, :], (128, 256))
            value = jnp.where(query_col < 8, left, right)
            fmask[t] = jnp.where(near, value, 0.0).astype(BF16)

    def make_coarse_mask():
        query = iota((64, 128), 0)
        key = iota((64, 128), 1)
        row_gap = key // 8 - 4 - query // 8
        col_gap = key % 8 - query % 8
        near = (row_gap <= 3) & (row_gap >= -3) & (col_gap <= 3) & (col_gap >= -3)
        value = jnp.broadcast_to(links[0:1, 0:128], (64, 128))
        cmask[...] = jnp.where(near, value, 0.0).astype(BF16)

    def make_fine_links():
        key = iota((1, 256), 1)
        key_row = key // 16
        key_tile = (key % 8) // 4
        for t in range(2):
            for c in range(2):
                row = jnp.zeros((1, 256), F32)
                for dy in range(3):
                    in_row = (key_row >= (0, 4, 12)[dy]) & (key_row < (4, 12, 16)[dy])
                    for kc in range(2):
                        link = fine_links[t, c, 3 * dy + kc - c + 1].astype(F32)
                        row = jnp.where(in_row & (key_tile == kc), link, row)
                links[2 * t + c : 2 * t + c + 1, :] = row

    def make_coarse_links():
        key_row = iota((1, 256), 1) // 8
        row = jnp.zeros((1, 256), F32)
        for dy in range(3):
            in_row = (key_row >= (0, 4, 12)[dy]) & (key_row < (4, 12, 16)[dy])
            row = jnp.where(in_row, coarse_links[0, 0, 3 * dy + 1].astype(F32), row)
        links[0:1, :] = row

    def halo_up():
        return remote(xs.at[:, pl.ds(16, 16), :], xs.at[:, pl.ds(80, 16), :], halo_s.at[0], halo_r.at[1], 0, b - 1)

    def halo_down():
        return remote(xs.at[:, pl.ds(64, 16), :], xs.at[:, pl.ds(0, 16), :], halo_s.at[1], halo_r.at[0], 0, b + 1)

    def link_copy(seg):
        return remote(links, links, link_s, link_r, seg, b)

    edges = has_up.astype(jnp.int32) + has_down.astype(jnp.int32)

    def scale_pixels():
        for m in range(MB):
            level = level_row(m)[:, 0:64]
            scaled = (frames[m] + level * noise[m]) * lax.rsqrt(level * level + 0.25)
            xs[m, 16:80, :] = jnp.concatenate([scaled, jnp.zeros((64, 64), F32)], axis=1)

        @pl.when(b == 0)
        def _():
            xs[:, 0:16, :] = jnp.zeros((MB, 16, 128), F32)

        @pl.when(b == n_space - 1)
        def _():
            xs[:, 80:96, :] = jnp.zeros((MB, 16, 128), F32)

    def make_embedding():
        entry = iota((256, 16), 0)
        pick = (iota((256, 16), 1) == 4 * (entry // 64) + entry % 4).astype(BF16)
        hi, low, _ = split3(patch_in[...])
        wide = dot_nn(pick, hi).astype(BF16)
        w3[0:256, :] = wide
        w3[256:512, :] = dot_nn(pick, low).astype(BF16)
        w3[512:768, :] = wide

    def transpose_weights(first, last, base):
        eye = (iota((G, G), 0) == iota((G, G), 1)).astype(BF16)

        def tile(i, carry):
            row = pl.multiple_of(i * G, G)
            col = pl.multiple_of((i - base) * G, G)
            for k in range(D // G):
                block = dot_nt(eye, w[pl.ds(row, G), k * G : (k + 1) * G])
                wt[k * G : (k + 1) * G, pl.ds(col, G)] = block.astype(BF16)
            return carry

        lax.fori_loop(first, last, tile, 0)

    def normed(value, m):
        scale = lax.rsqrt(jnp.mean(value * value, axis=-1, keepdims=True) + EPS)
        return (value * scale * gains[pl.ds(m, 1), :]).astype(BF16)

    def embed(rows4):
        flat = jnp.concatenate(
            [rows4[0] + pltpu.roll(rows4[1], 64, 1), rows4[2] + pltpu.roll(rows4[3], 64, 1)], axis=1
        )
        hi, low, _ = split3(flat)
        token = iota((16, 256), 0)
        col = iota((16, 256), 1)
        own = ((col % 64) // 4 == 2 * (token % 8) + token // 8).astype(F32)
        count = flat.shape[0]

        def spread(piece):
            wide = jnp.broadcast_to(piece.astype(F32)[:, None, :], (count, 16, 256)) * own[None]
            return wide.reshape(count * 16, 256).astype(BF16)

        first = spread(hi)
        return dot_nn(jnp.concatenate([first, first, spread(low)], axis=1), w3[...])

    def run_jobs(jobs):
        def finish(block, part, g, put):
            if part < 2:
                power = dot_nn((block * block).astype(BF16), head_mean)
                block = block * lax.rsqrt(power + EPS)
            if part == 0:
                block = block * qscale[g : g + 1, :]
            put(block.astype(BF16))

        pending = []
        for make, part, g, put in jobs:
            pending.append((make(), part, g, put))
            if len(pending) > 2:
                finish(*pending.pop(0))
        for job in pending:
            finish(*job)

    def fine_jobs(source, first, count, parts, put):
        jobs = []
        for part in parts:
            for g in range(FI // G):
                at = part * FI + g * G
                lo, n = (first, count) if part == 0 else (0, source.shape[0])
                jobs.append(
                    (
                        lambda at=at, lo=lo, n=n: dot_nt(source[lo : lo + n, :], w[at : at + G, :]),
                        part, g, functools.partial(put, part, g),
                    )
                )
        return jobs

    def embed_own(m):
        own = embed([xs[m, pl.ds(16 + a, 16, stride=4), :] for a in range(4)])
        x[m, 2:10] = own.reshape(8, 2, 2, 8, D)
        nrm[m * OWN : (m + 1) * OWN, :] = normed(own, m)

    def project_own(m):
        def put(part, g, block):
            if part == 0:
                q_s[2 * m + g, :, :] = block
            else:
                (k_s if part == 1 else v_s)[2 * m + g, 64:320, :] = block

        own = nrm.at[pl.ds(pl.multiple_of(m * OWN, OWN), OWN), :]
        run_jobs(fine_jobs(own, 0, OWN, (0, 1, 2), put))

    def project_halo(m):
        rows4 = [
            jnp.concatenate([xs[m, pl.ds(a, 4, stride=4), :], xs[m, pl.ds(80 + a, 4, stride=4), :]], axis=0)
            for a in range(4)
        ]
        halo[...] = normed(embed(rows4), m)

        def put(part, g, block):
            dst = k_s if part == 1 else v_s
            dst[2 * m + g, 0:64, :] = block[0:64]
            dst[2 * m + g, 320:384, :] = block[64:128]

        run_jobs(fine_jobs(halo, 0, 128, (1, 2), put))

    def widen(m):
        coarse = cin[m, 16:112, :]
        for a in range(2):
            for c in range(2):
                at = (2 * a + c) * D
                x[m, :, a, c] += dot_nn(coarse, wt[:, at : at + D]).reshape(12, 8, D)

    def embed_all(m):
        embedded = embed([xs[m, pl.ds(a, 24, stride=4), :] for a in range(4)])
        x[m] = embedded.reshape(12, 2, 2, 8, D)

    def make_skip(m):
        whole = (x[m].reshape(FINE, D) + dot_nn(mixed[m], wo[...])).astype(BF16)
        x[m] = whole.astype(F32).reshape(12, 2, 2, 8, D)

    def project_fine(m):
        nrm[0:FINE, :] = normed(x[m].reshape(FINE, D), m)

        def put(part, g, block):
            (q_s, k_s, v_s)[part][2 * m + g, :, :] = block

        run_jobs(fine_jobs(nrm.at[0:FINE], 64, OWN, (0, 1, 2), put))

    def attend(items, lags):
        held = [{} for _ in items]

        def score(i):
            queries, keys = items[i][0](), items[i][1]()
            head = iota(queries.shape, 1) // 64
            stacked = jnp.concatenate(
                [jnp.where(head == h, queries, jnp.zeros_like(queries)) for h in range(4)], axis=0
            )
            held[i]["score"] = dot_nt(stacked, keys)

        def weigh(i):
            expo = jnp.exp2(held[i].pop("score")).astype(BF16)
            held[i]["expo"] = expo * jnp.concatenate([items[i][3]()] * 4, axis=0)

        def gather(i):
            expo = held[i].pop("expo")
            held[i]["sum"] = jnp.sum(expo.astype(F32), axis=-1, keepdims=True)
            held[i]["mixed"] = dot_nn(expo, items[i][2]())

        def place_heads(i):
            total, value = held[i].pop("sum"), held[i].pop("mixed")
            count = value.shape[0] // 4
            part = [value[h * count : (h + 1) * count] for h in range(4)]
            sums = [total[h * count : (h + 1) * count] for h in range(4)]
            first = iota((count, 128), 1) < 64
            number = jnp.concatenate(
                [
                    jnp.where(first, part[0][:, 0:128], part[1][:, 0:128]),
                    jnp.where(first, part[2][:, 128:256], part[3][:, 128:256]),
                ],
                axis=1,
            )
            weight = jnp.concatenate(
                [jnp.where(first, sums[0], sums[1]), jnp.where(first, sums[2], sums[3])], axis=1
            )
            items[i][4]((number / weight).astype(BF16))

        stages = (score, weigh, gather, place_heads)
        for step in range(len(items) + lags[-1]):
            for stage, lag in zip(stages, lags):
                if 0 <= step - lag < len(items):
                    stage(step - lag)

    def mix_fine(m):
        items = []
        for t in range(2):
            for g in range(2):
                rows, near, cols = pl.ds(128 * t, 128), pl.ds(128 * t, 256), pl.ds(g * G, G)

                def put(value, rows=rows, cols=cols):
                    mix[m, rows, cols] = value

                items.append(
                    (
                        lambda g=g, rows=rows: q_s[2 * m + g, rows, :],
                        lambda g=g, near=near: k_s[2 * m + g, near, :],
                        lambda g=g, near=near: v_s[2 * m + g, near, :],
                        lambda t=t: fmask[t],
                        put,
                    )
                )
        attend(items, (0, 1, 1, 2))

    def add_fine(m):
        update = dot_nn(mix[m], w[3 * FI : 4 * FI, :])
        x[m, 2:10] += update.reshape(8, 2, 2, 8, D)

    def coarse_jobs(first, count, parts):
        jobs = []
        for part in parts:
            for g in range(CI // G):
                at = part * CI + g * G

                def put(block, part=part, g=g):
                    (q_s, k_s, v_s)[part][g, 0:count, :] = block

                jobs.append(
                    (lambda at=at: dot_nn(nrm[first : first + count, :], wt[:, at : at + G]), part, g, put)
                )
        return jobs

    def coarse_queries(m):
        nrm[32:96, :] = normed(cin[m, 32:96, :].astype(F32), m)
        run_jobs(coarse_jobs(32, COWN, (0,)))

    def coarse_rest(m):
        for i in range(2):
            edge = edge_in[m, i].astype(F32)
            edge = jnp.concatenate([edge[0:24], edge[24:48]], axis=1)
            at = (8, 96)[i]
            nrm[at : at + 24, :] = normed(edge, m)
        run_jobs(coarse_jobs(0, COARSE, (1, 2)))
        items = []
        for g in range(6):

            def put(value, g=g):
                grp[:, g * G : (g + 1) * G] = value

            items.append(
                (
                    lambda g=g: q_s[g, 0:COWN, :],
                    lambda g=g: k_s[g, 0:COARSE, :],
                    lambda g=g: v_s[g, 0:COARSE, :],
                    lambda: cmask[...],
                    put,
                )
            )
        attend(items, (0, 1, 2, 3))
        update = dot_nn(grp[:, 0:CI], w[3 * CI : 4 * CI, :])
        put_coarse(m, cin[m, 32:96, :].astype(F32) + update)

    def put_coarse(m, result):
        cout[m] = result.astype(BF16)
        for i in range(2):
            rows = result[0:24] if i == 0 else result[40:64]
            edge_out[m, i] = jnp.concatenate([rows[:, 0:512], rows[:, 512:1024]], axis=0).astype(BF16)

    def merge(m):
        own = x[m, 2:10]
        for a in range(2):
            for c in range(2):
                at = (2 * a + c) * D
                grp[:, at : at + D] = own[:, a, c].reshape(COWN, D).astype(BF16)
        put_coarse(m, dot_nn(grp[...], w[4 * FI :, :]))

    def head(m):
        top = x[m, 2:10].reshape(OWN, D)
        scale = lax.rsqrt(jnp.mean(top * top, axis=-1, keepdims=True) + EPS)
        pixels = dot_nn((top * scale).astype(BF16), pox[...])
        token = iota((16, 256), 0)
        col = iota((16, 256), 1)
        own = 2 * (token % 8) + token // 8 == 4 * (col // 64) + (col // 4) % 4
        spread = jnp.where(own[None], pixels.reshape(16, 16, 256), 0.0)
        total = jnp.sum(spread, axis=1)
        pixout[m, 0] = total[:, 0:128]
        pixout[m, 1] = total[:, 128:256]

    def coarse_own(m, seg):
        return remote(cout.at[m], cin.at[m, pl.ds(32, 64), :], c_s.at[m, 0], c_r.at[m, 0], seg + 1, b)

    def edge_up(m, seg):
        if seg < 2:
            src, dst = edge_out.at[m, 0], edge_in.at[m, 1]
        else:
            src, dst = cout.at[m, pl.ds(0, 16), :], cin.at[m, pl.ds(96, 16), :]
        return remote(src, dst, c_s.at[m, 1], c_r.at[m, 2], seg + 1, b - 1)

    def edge_down(m, seg):
        if seg < 2:
            src, dst = edge_out.at[m, 1], edge_in.at[m, 0]
        else:
            src, dst = cout.at[m, pl.ds(48, 16), :], cin.at[m, pl.ds(16, 16), :]
        return remote(src, dst, c_s.at[m, 2], c_r.at[m, 1], seg + 1, b + 1)

    def send_coarse(m, seg, act):
        act(coarse_own(m, seg))

        @pl.when(has_up)
        def _():
            act(edge_up(m, seg))

        @pl.when(has_down)
        def _():
            act(edge_down(m, seg))

    def take_own(m):
        arrived(cin.at[m, pl.ds(32, 64), :], c_r.at[m, 0])

    def take_edges(m, above, below):
        @pl.when(has_up)
        def _():
            arrived(above, c_r.at[m, 1])

        @pl.when(has_down)
        def _():
            arrived(below, c_r.at[m, 2])

    def pixels_on():
        return remote(xs, xs, xs_s, xs_r, 3, b)

    def half(which):
        return wo.at[pl.ds(pl.multiple_of(which * 256, 256), 256), :]

    mine, other = b % 2, 1 - b % 2

    def half_copy():
        rows = pl.ds(pl.multiple_of(3 * FI + mine * 256, 256), 256)
        return pltpu.make_async_copy(w_hbm.at[0, rows, :], half(mine), in_sem.at[6])

    def weights_on(seg):
        return remote(half(mine), half(mine), wo_s, wo_r, seg, b)

    def weights_across():
        return remote(half(mine), half(mine), wx_s, wx_r, 3, b + 1 - 2 * mine)

    def mix_copy(m):
        return remote(mix.at[m], mixed.at[m, pl.ds(64, OWN), :], mix_s.at[m], mix_r.at[m], 3, b)

    def mix_up(m):
        return remote(
            mixed.at[m, pl.ds(64, 64), :], mixed.at[m, pl.ds(320, 64), :], fwd_s.at[m, 0], fwd_r.at[m, 1], 3, b - 1
        )

    def mix_down(m):
        return remote(
            mixed.at[m, pl.ds(256, 64), :], mixed.at[m, pl.ds(0, 64), :], fwd_s.at[m, 1], fwd_r.at[m, 0], 3, b + 1
        )

    def forward_mix(m, act):
        @pl.when(has_up)
        def _():
            act(mix_up(m))

        @pl.when(has_down)
        def _():
            act(mix_down(m))

    def pixel_copy(m, seg):
        return pltpu.make_async_remote_copy(
            src_ref=pixout.at[m, seg // 2], dst_ref=pixin.at[m], send_sem=pix_s.at[m, seg], recv_sem=pix_r.at[m],
            device_id=(seg, b), device_id_type=pl.DeviceIdType.MESH,
        )

    def start(copy):
        copy.start()

    def sent(copy):
        copy.wait_send()

    def take_gains():
        freq_copy.wait()
        cond_copy.wait()
        make_gains()

    @pl.when(s == 0)
    def _():
        frame_copy.wait()
        noise_copy.wait()
        scale_pixels()
        pl.semaphore_wait(barrier, 2 + 2 * edges)

        @pl.when(has_up)
        def _():
            halo_up().start()

        @pl.when(has_down)
        def _():
            halo_down().start()

        half_copy().start()
        make_fine_links()
        link_copy(3).start()
        take_gains()
        patch_in_copy.wait()
        make_embedding()
        embed_own(0)
        half_copy().wait()
        weights_on(1).start()
        weight_copy(0).wait()
        for i in range(1, CHUNKS):
            weight_copy(i).start()
        project_own(0)
        make_fine_mask()

        @pl.when(has_up)
        def _():
            arrived(xs.at[:, pl.ds(0, 16), :], halo_r.at[0])

        @pl.when(has_down)
        def _():
            arrived(xs.at[:, pl.ds(80, 16), :], halo_r.at[1])

        pixels_on().start()
        for m in range(MB):
            if m > 0:
                embed_own(m)
                project_own(m)
            project_halo(m)
            mix_fine(m)
            if m == 0:
                for i in range(1, CHUNKS):
                    weight_copy(i).wait()
            add_fine(m)
            merge(m)
            send_coarse(m, 0, start)
            mix_copy(m).start()

    @pl.when((s == 1) | (s == 2))
    def _():
        nrm[0:8, :] = jnp.zeros((8, D), BF16)
        nrm[120:128, :] = jnp.zeros((8, D), BF16)

        @pl.when(b == 0)
        def _():
            edge_in[:, 0] = jnp.zeros((MB, 48, 512), BF16)

        @pl.when(b == n_space - 1)
        def _():
            edge_in[:, 1] = jnp.zeros((MB, 48, 512), BF16)

        @pl.when(s == 1)
        def _():
            make_coarse_links()
            pl.semaphore_wait(barrier, 2 + edges)
            link_copy(2).start()
            arrived(half(mine), wo_r)
            weights_on(3).start()

        @pl.when(s == 2)
        def _():
            pl.semaphore_wait(barrier, 1 + edges)
            arrived(links, link_r)

        make_coarse_mask()
        take_gains()
        for i in range(3):
            weight_copy(i).wait()
            transpose_weights(6 * i, 6 * i + 6, 0)
        weight_copy(3).wait()

        def one_batch(m, carry):
            take_own(m)
            coarse_queries(m)
            take_edges(m, edge_in.at[m, 0], edge_in.at[m, 1])
            coarse_rest(m)

            @pl.when(s == 1)
            def _():
                send_coarse(m, 1, start)

            @pl.when(s == 2)
            def _():
                send_coarse(m, 2, start)

            return carry

        lax.fori_loop(0, MB, one_batch, 0)

    @pl.when(s == 3)
    def _():
        @pl.when(b == 0)
        def _():
            cin[:, 16:32, :] = jnp.zeros((MB, 16, D), BF16)
            mixed[:, 0:64, :] = jnp.zeros((MB, 64, FI), BF16)

        @pl.when(b == n_space - 1)
        def _():
            cin[:, 96:112, :] = jnp.zeros((MB, 16, D), BF16)
            mixed[:, 320:384, :] = jnp.zeros((MB, 64, FI), BF16)

        take_gains()
        patch_in_copy.wait()
        make_embedding()
        patch_out_copy.wait()
        entry = iota((16, 256), 0)
        col = iota((16, 256), 1)
        pick = (entry == 4 * ((col // 16) % 4) + col % 4).astype(BF16)
        pox[...] = lax.dot_general(
            patch_out[...], pick, (((0,), (0,)), ((), ())), preferred_element_type=F32
        ).astype(BF16)
        weight_copy(0).wait()
        weight_copy(1).wait()
        transpose_weights(8, 12, 8)
        weight_copy(2).wait()
        transpose_weights(12, 18, 8)
        weight_copy(3).wait()
        transpose_weights(18, 24, 8)
        pl.semaphore_wait(barrier, 4 + edges)
        arrived(links, link_r)
        make_fine_mask()
        arrived(half(mine), wo_r)
        weights_across().start()
        arrived(xs, xs_r)
        for m in range(MB):
            embed_all(m)
        arrived(half(other), wx_r)
        for m in range(MB):
            arrived(mixed.at[m, pl.ds(64, OWN), :], mix_r.at[m])
            forward_mix(m, start)
        for m in range(MB):

            @pl.when(has_up)
            def _():
                arrived(mixed.at[m, pl.ds(0, 64), :], fwd_r.at[m, 0])

            @pl.when(has_down)
            def _():
                arrived(mixed.at[m, pl.ds(320, 64), :], fwd_r.at[m, 1])

            make_skip(m)

        def one_batch(m, carry):
            take_own(m)
            take_edges(m, cin.at[m, pl.ds(16, 16), :], cin.at[m, pl.ds(96, 16), :])
            widen(m)
            project_fine(m)
            mix_fine(m)
            add_fine(m)
            head(m)
            for seg in range(4):
                pixel_copy(m, seg).start()
            return carry

        lax.fori_loop(0, MB, one_batch, 0)

    for m in range(MB):
        arrived(pixin.at[m], pix_r.at[m])
        pixels = pixin[m]
        pixels = jnp.where(s % 2 == 1, pltpu.roll(pixels, 64, 1), pixels)
        for a in range(4):
            placed[pl.ds(a, 16, stride=4), :] = pltpu.roll(pixels, (128 - 16 * a) % 128, 1)
        out[m] = placed[...].T[0:16, :]

    @pl.when(s == 0)
    def _():
        @pl.when(has_up)
        def _():
            halo_up().wait_send()

        @pl.when(has_down)
        def _():
            halo_down().wait_send()

        link_copy(3).wait_send()
        for m in range(MB):
            send_coarse(m, 0, sent)
            mix_copy(m).wait_send()
        weights_on(1).wait_send()
        pixels_on().wait_send()

    @pl.when(s == 1)
    def _():
        link_copy(2).wait_send()
        weights_on(3).wait_send()
        for m in range(MB):
            send_coarse(m, 1, sent)

    @pl.when(s == 2)
    def _():
        for m in range(MB):
            send_coarse(m, 2, sent)

    @pl.when(s == 3)
    def _():
        weights_across().wait_send()
        for m in range(MB):
            forward_mix(m, sent)
            for seg in range(4):
                pixel_copy(m, seg).wait_send()


def per_device(
    clean_frames, noise, noise_steps, noise_freqs, cond_weights, patch_in, patch_out, section_weights, head_scales,
    fine_links, coarse_links,
):
    vmem = pl.BlockSpec(memory_space=pltpu.VMEM)
    smem = pl.BlockSpec(memory_space=pltpu.SMEM)
    hbm = pl.BlockSpec(memory_space=pl.ANY)
    dma = pltpu.SemaphoreType.DMA
    placed = pl.pallas_call(
        functools.partial(kernel, lax.axis_size("space")),
        out_shape=jax.ShapeDtypeStruct((MB, 16, 64), F32),
        in_specs=[hbm, hbm, smem, hbm, hbm, hbm, hbm, hbm, smem, smem, smem],
        out_specs=vmem,
        scratch_shapes=[
            pltpu.VMEM((6144, D), BF16),
            pltpu.VMEM((D, 3 * CI), BF16),
            pltpu.VMEM((MB, 64, 64), F32),
            pltpu.VMEM((MB, 64, 64), F32),
            pltpu.VMEM((128,), F32),
            pltpu.VMEM((1, 256, D), BF16),
            pltpu.VMEM((16, D), F32),
            pltpu.VMEM((16, D), BF16),
            pltpu.VMEM((MB, 96, 128), F32),
            pltpu.VMEM((MB, 12, 2, 2, 8, D), F32),
            pltpu.VMEM((2 * OWN, D), BF16),
            pltpu.VMEM((128, D), BF16),
            pltpu.VMEM((6, OWN, G), BF16),
            pltpu.VMEM((6, FINE, G), BF16),
            pltpu.VMEM((6, FINE, G), BF16),
            pltpu.VMEM((MB, OWN, FI), BF16),
            pltpu.VMEM((MB, FINE, FI), BF16),
            pltpu.VMEM((COWN, 4 * D), BF16),
            pltpu.VMEM((FI, D), BF16),
            pltpu.VMEM((MB, COARSE, D), BF16),
            pltpu.VMEM((MB, COWN, D), BF16),
            pltpu.VMEM((MB, 2, 48, 512), BF16),
            pltpu.VMEM((MB, 2, 48, 512), BF16),
            pltpu.VMEM((768, D), BF16),
            pltpu.VMEM((D, 256), BF16),
            pltpu.VMEM((8, D), F32),
            pltpu.VMEM((8, G), F32),
            pltpu.VMEM((8, 256), F32),
            pltpu.VMEM((2, 128, 256), BF16),
            pltpu.VMEM((64, 128), BF16),
            pltpu.VMEM((MB, 2, 16, 128), F32),
            pltpu.VMEM((MB, 16, 128), F32),
            pltpu.VMEM((64, 128), F32),
            dma((CHUNKS,)),
            dma((7,)),
            dma((2,)), dma((2,)),
            dma(()), dma(()),
            dma((MB, 3)), dma((MB, 3)),
            dma(()), dma(()),
            dma(()), dma(()),
            dma(()), dma(()),
            dma((MB,)), dma((MB,)),
            dma((MB, 2)), dma((MB, 2)),
            dma((MB, 4)), dma((MB,)),
        ],
        compiler_params=pltpu.CompilerParams(
            collective_id=0, has_side_effects=True, vmem_limit_bytes=58 << 20
        ),
    )(
        clean_frames, noise, noise_steps, noise_freqs, cond_weights, patch_in, patch_out.T, section_weights,
        head_scales, fine_links, coarse_links,
    )
    return placed.transpose(0, 2, 1)


def solution(mesh):
    in_specs = (
        P(None, "space", None),
        P(None, "space", None),
        P(),
        P(),
        P("segment", None, None),
        P(),
        P(),
        P("segment", None, None),
        P("segment", None),
        P("space", None, None),
        P("space", None, None),
    )
    out_specs = P(None, "space", "segment")
    return jax.shard_map(
        per_device, mesh=mesh, in_specs=in_specs, out_specs=out_specs, check_vma=False
    )
```

```python
import functools
import math

import jax
import jax.numpy as jnp
from jax import lax
from jax.experimental import pallas as pl
from jax.experimental.pallas import tpu as pltpu
from jax.sharding import PartitionSpec as P

STEPS = 1000
MB = 2
D = 1024
FI = 512
CI = 1536
G = 256
OWN = 256
FINE = 384
COWN = 64
COARSE = 128
EPS = 1e-06

LOG_LOW = math.log(0.002)
LOG_HIGH = math.log(80.0)
LOG2E = 1.0 / math.log(2.0)

F32 = jnp.float32
BF16 = jnp.bfloat16
NT = (((1,), (1,)), ((), ()))
NN = (((1,), (0,)), ((), ()))

CHUNK = 1536
CHUNKS = 4


def dot_nt(a, b):
    return lax.dot_general(a, b, NT, preferred_element_type=F32)


def dot_nn(a, b):
    return lax.dot_general(a, b, NN, preferred_element_type=F32)


def iota(shape, dim):
    return lax.broadcasted_iota(jnp.int32, shape, dim)


def split3(value):
    hi = value.astype(BF16)
    rest = value - hi.astype(F32)
    mid = rest.astype(BF16)
    return hi, mid, (rest - mid.astype(F32)).astype(BF16)


def kernel(
    n_space,
    frames_hbm, noise_hbm, steps, freqs_hbm, cond_hbm, patch_in_hbm, patch_out_hbm, w_hbm, scales, fine_links,
    coarse_links,
    out,
    w, wt, frames, noise, freqs, cond, patch_in, patch_out, xs, x, nrm, halo, q_s, k_s, v_s, mix, mixed, grp, wo, cin, cout,
    edge_out, edge_in, w3, pox, gains, qscale, links, fmask, cmask, pixout, pixin, placed,
    w_sem, in_sem, halo_s, halo_r, link_s, link_r, c_s, c_r, xs_s, xs_r, wo_s, wo_r, wx_s, wx_r, mix_s, mix_r, fwd_s,
    fwd_r, pix_s, pix_r,
):
    s = lax.axis_index("segment")
    p = lax.axis_index("space")
    b = p + (s // 2) * (1 - 2 * (p % 2))
    has_up = b > 0
    has_down = b < n_space - 1

    def place(seg, block):
        return block + (seg // 2) * (1 - 2 * (block % 2))

    def remote(src, dst, ssem, rsem, seg, block):
        return pltpu.make_async_remote_copy(
            src_ref=src, dst_ref=dst, send_sem=ssem, recv_sem=rsem,
            device_id=(seg, place(seg, block)), device_id_type=pl.DeviceIdType.MESH,
        )

    def arrived(dst, rsem):
        pltpu.make_async_remote_copy(
            src_ref=dst, dst_ref=dst, send_sem=rsem, recv_sem=rsem,
            device_id=(s, p), device_id_type=pl.DeviceIdType.MESH,
        ).wait_recv()

    def weight_copy(i):
        rows = pl.ds(i * CHUNK, CHUNK)
        return pltpu.make_async_copy(w_hbm.at[0, rows, :], w.at[rows, :], w_sem.at[i])

    freq_copy = pltpu.make_async_copy(freqs_hbm, freqs, in_sem.at[0])
    cond_copy = pltpu.make_async_copy(cond_hbm, cond, in_sem.at[1])
    frame_copy = pltpu.make_async_copy(frames_hbm, frames, in_sem.at[2])
    noise_copy = pltpu.make_async_copy(noise_hbm, noise, in_sem.at[3])
    patch_in_copy = pltpu.make_async_copy(patch_in_hbm, patch_in, in_sem.at[4])
    patch_out_copy = pltpu.make_async_copy(patch_out_hbm, patch_out, in_sem.at[5])

    barrier = pltpu.get_barrier_semaphore()

    def greet(seg, space):
        pl.semaphore_signal(barrier, inc=1, device_id=(seg, space), device_id_type=pl.DeviceIdType.MESH)

    @pl.when((s == 0) | (s == 3))
    def _():
        @pl.when(has_up)
        def _():
            greet(s, place(s, b - 1))

        @pl.when(has_down)
        def _():
            greet(s, place(s, b + 1))

    @pl.when(s == 0)
    def _():
        frame_copy.start()
        noise_copy.start()

    @pl.when((s == 0) | (s == 3))
    def _():
        patch_in_copy.start()

    freq_copy.start()
    cond_copy.start()
    weight_copy(0).start()

    @pl.when(s > 0)
    def _():
        for i in range(1, CHUNKS):
            weight_copy(i).start()

    greet(3, place(3, p))

    @pl.when(s > 0)
    def _():
        greet(s - 1, place(s - 1, b))

        @pl.when(has_up)
        def _():
            greet(s - 1, place(s - 1, b - 1))

        @pl.when(has_down)
        def _():
            greet(s - 1, place(s - 1, b + 1))

    @pl.when(s == 3)
    def _():
        greet(0, b)
        greet(1, b)
        patch_out_copy.start()

    def level_row(m):
        step = jnp.full((1, 128), steps[m], jnp.int32).astype(F32)
        return jnp.exp(LOG_LOW + step / (STEPS - 1) * (LOG_HIGH - LOG_LOW))

    lane = iota((1, G), 1) // 64
    for g in range(6):
        four = [scales[0, 4 * g + h] for h in range(4)]
        row = jnp.where(lane == 0, four[0], jnp.where(lane == 1, four[1], jnp.where(lane == 2, four[2], four[3])))
        qscale[g : g + 1, :] = row * (LOG2E / 64.0)

    head_mean = jnp.where(iota((G, G), 0) // 64 == iota((G, G), 1) // 64, 1.0 / 64.0, 0.0).astype(BF16)

    def make_gains():
        rows = []
        for m in range(MB):
            phases = 2.0 * math.pi * (jnp.log(level_row(m)) / 4.0) * freqs[...].reshape(1, 128)
            rows.append(jnp.concatenate([jnp.cos(phases), jnp.sin(phases)], axis=1))
        features = jnp.concatenate(rows + [jnp.zeros((6, 256), F32)], axis=0)
        hi, mid, low = split3(features)
        gains[...] = 1.0 + (dot_nn(hi, cond[0]) + dot_nn(mid, cond[0]) + dot_nn(low, cond[0]))

    def make_fine_mask():
        query = iota((128, 256), 0)
        key = iota((128, 256), 1)
        row_gap = key // 16 - 4 - query // 16
        query_col = 2 * (query % 8) + (query // 8) % 2
        key_col = 2 * (key % 8) + (key // 8) % 2
        col_gap = key_col - query_col
        near = (row_gap <= 3) & (row_gap >= -3) & (col_gap <= 3) & (col_gap >= -3)
        for t in range(2):
            left = jnp.broadcast_to(links[2 * t : 2 * t + 1, :], (128, 256))
            right = jnp.broadcast_to(links[2 * t + 1 : 2 * t + 2, :], (128, 256))
            value = jnp.where(query_col < 8, left, right)
            fmask[t] = jnp.where(near, value, 0.0).astype(BF16)

    def make_coarse_mask():
        query = iota((64, 128), 0)
        key = iota((64, 128), 1)
        row_gap = key // 8 - 4 - query // 8
        col_gap = key % 8 - query % 8
        near = (row_gap <= 3) & (row_gap >= -3) & (col_gap <= 3) & (col_gap >= -3)
        value = jnp.broadcast_to(links[0:1, 0:128], (64, 128))
        cmask[...] = jnp.where(near, value, 0.0).astype(BF16)

    def make_fine_links():
        key = iota((1, 256), 1)
        key_row = key // 16
        key_tile = (key % 8) // 4
        for t in range(2):
            for c in range(2):
                row = jnp.zeros((1, 256), F32)
                for dy in range(3):
                    in_row = (key_row >= (0, 4, 12)[dy]) & (key_row < (4, 12, 16)[dy])
                    for kc in range(2):
                        link = fine_links[t, c, 3 * dy + kc - c + 1].astype(F32)
                        row = jnp.where(in_row & (key_tile == kc), link, row)
                links[2 * t + c : 2 * t + c + 1, :] = row

    def make_coarse_links():
        key_row = iota((1, 256), 1) // 8
        row = jnp.zeros((1, 256), F32)
        for dy in range(3):
            in_row = (key_row >= (0, 4, 12)[dy]) & (key_row < (4, 12, 16)[dy])
            row = jnp.where(in_row, coarse_links[0, 0, 3 * dy + 1].astype(F32), row)
        links[0:1, :] = row

    def halo_up():
        return remote(xs.at[:, pl.ds(16, 16), :], xs.at[:, pl.ds(80, 16), :], halo_s.at[0], halo_r.at[1], 0, b - 1)

    def halo_down():
        return remote(xs.at[:, pl.ds(64, 16), :], xs.at[:, pl.ds(0, 16), :], halo_s.at[1], halo_r.at[0], 0, b + 1)

    def link_copy(seg):
        return remote(links, links, link_s, link_r, seg, b)

    edges = has_up.astype(jnp.int32) + has_down.astype(jnp.int32)

    def scale_pixels():
        for m in range(MB):
            level = level_row(m)[:, 0:64]
            scaled = (frames[m] + level * noise[m]) * lax.rsqrt(level * level + 0.25)
            xs[m, 16:80, :] = jnp.concatenate([scaled, jnp.zeros((64, 64), F32)], axis=1)

        @pl.when(b == 0)
        def _():
            xs[:, 0:16, :] = jnp.zeros((MB, 16, 128), F32)

        @pl.when(b == n_space - 1)
        def _():
            xs[:, 80:96, :] = jnp.zeros((MB, 16, 128), F32)

    def make_embedding():
        entry = iota((256, 16), 0)
        pick = (iota((256, 16), 1) == 4 * (entry // 64) + entry % 4).astype(BF16)
        hi, low, _ = split3(patch_in[...])
        wide = dot_nn(pick, hi).astype(BF16)
        w3[0:256, :] = wide
        w3[256:512, :] = dot_nn(pick, low).astype(BF16)
        w3[512:768, :] = wide

    def transpose_weights(first, last, base):
        eye = (iota((G, G), 0) == iota((G, G), 1)).astype(BF16)

        def tile(i, carry):
            row = pl.multiple_of(i * G, G)
            col = pl.multiple_of((i - base) * G, G)
            for k in range(D // G):
                block = dot_nt(eye, w[pl.ds(row, G), k * G : (k + 1) * G])
                wt[k * G : (k + 1) * G, pl.ds(col, G)] = block.astype(BF16)
            return carry

        lax.fori_loop(first, last, tile, 0)

    def normed(value, m):
        scale = lax.rsqrt(jnp.mean(value * value, axis=-1, keepdims=True) + EPS)
        return (value * scale * gains[pl.ds(m, 1), :]).astype(BF16)

    def embed(rows4):
        flat = jnp.concatenate(
            [rows4[0] + pltpu.roll(rows4[1], 64, 1), rows4[2] + pltpu.roll(rows4[3], 64, 1)], axis=1
        )
        hi, low, _ = split3(flat)
        token = iota((16, 256), 0)
        col = iota((16, 256), 1)
        own = ((col % 64) // 4 == 2 * (token % 8) + token // 8).astype(F32)
        count = flat.shape[0]

        def spread(piece):
            wide = jnp.broadcast_to(piece.astype(F32)[:, None, :], (count, 16, 256)) * own[None]
            return wide.reshape(count * 16, 256).astype(BF16)

        first = spread(hi)
        return dot_nn(jnp.concatenate([first, first, spread(low)], axis=1), w3[...])

    def run_jobs(jobs):
        def finish(block, part, g, put):
            if part < 2:
                power = dot_nn((block * block).astype(BF16), head_mean)
                block = block * lax.rsqrt(power + EPS)
            if part == 0:
                block = block * qscale[g : g + 1, :]
            put(block.astype(BF16))

        pending = []
        for make, part, g, put in jobs:
            pending.append((make(), part, g, put))
            if len(pending) > 2:
                finish(*pending.pop(0))
        for job in pending:
            finish(*job)

    def fine_jobs(source, first, count, parts, put):
        jobs = []
        for part in parts:
            for g in range(FI // G):
                at = part * FI + g * G
                lo, n = (first, count) if part == 0 else (0, source.shape[0])
                jobs.append(
                    (
                        lambda at=at, lo=lo, n=n: dot_nt(source[lo : lo + n, :], w[at : at + G, :]),
                        part, g, functools.partial(put, part, g),
                    )
                )
        return jobs

    def embed_own(m):
        own = embed([xs[m, pl.ds(16 + a, 16, stride=4), :] for a in range(4)])
        x[m, 2:10] = own.reshape(8, 2, 2, 8, D)
        nrm[m * OWN : (m + 1) * OWN, :] = normed(own, m)

    def project_own(m):
        def put(part, g, block):
            if part == 0:
                q_s[2 * m + g, :, :] = block
            else:
                (k_s if part == 1 else v_s)[2 * m + g, 64:320, :] = block

        own = nrm.at[pl.ds(pl.multiple_of(m * OWN, OWN), OWN), :]
        run_jobs(fine_jobs(own, 0, OWN, (0, 1, 2), put))

    def project_halo(m):
        rows4 = [
            jnp.concatenate([xs[m, pl.ds(a, 4, stride=4), :], xs[m, pl.ds(80 + a, 4, stride=4), :]], axis=0)
            for a in range(4)
        ]
        halo[...] = normed(embed(rows4), m)

        def put(part, g, block):
            dst = k_s if part == 1 else v_s
            dst[2 * m + g, 0:64, :] = block[0:64]
            dst[2 * m + g, 320:384, :] = block[64:128]

        run_jobs(fine_jobs(halo, 0, 128, (1, 2), put))

    def widen(m):
        coarse = cin[m, 16:112, :]
        for a in range(2):
            for c in range(2):
                at = (2 * a + c) * D
                x[m, :, a, c] += dot_nn(coarse, wt[:, at : at + D]).reshape(12, 8, D)

    def embed_all(m):
        embedded = embed([xs[m, pl.ds(a, 24, stride=4), :] for a in range(4)])
        x[m] = embedded.reshape(12, 2, 2, 8, D)

    def make_skip(m):
        whole = (x[m].reshape(FINE, D) + dot_nn(mixed[m], wo[...])).astype(BF16)
        x[m] = whole.astype(F32).reshape(12, 2, 2, 8, D)

    def project_fine(m):
        nrm[0:FINE, :] = normed(x[m].reshape(FINE, D), m)

        def put(part, g, block):
            (q_s, k_s, v_s)[part][2 * m + g, :, :] = block

        run_jobs(fine_jobs(nrm.at[0:FINE], 64, OWN, (0, 1, 2), put))

    def attend(items, lags):
        held = [{} for _ in items]

        def score(i):
            queries, keys = items[i][0](), items[i][1]()
            head = iota(queries.shape, 1) // 64
            stacked = jnp.concatenate(
                [jnp.where(head == h, queries, jnp.zeros_like(queries)) for h in range(4)], axis=0
            )
            held[i]["score"] = dot_nt(stacked, keys)

        def weigh(i):
            expo = jnp.exp2(held[i].pop("score")).astype(BF16)
            held[i]["expo"] = expo * jnp.concatenate([items[i][3]()] * 4, axis=0)

        def gather(i):
            expo = held[i].pop("expo")
            held[i]["sum"] = jnp.sum(expo.astype(F32), axis=-1, keepdims=True)
            held[i]["mixed"] = dot_nn(expo, items[i][2]())

        def place_heads(i):
            total, value = held[i].pop("sum"), held[i].pop("mixed")
            count = value.shape[0] // 4
            part = [value[h * count : (h + 1) * count] for h in range(4)]
            sums = [total[h * count : (h + 1) * count] for h in range(4)]
            first = iota((count, 128), 1) < 64
            number = jnp.concatenate(
                [
                    jnp.where(first, part[0][:, 0:128], part[1][:, 0:128]),
                    jnp.where(first, part[2][:, 128:256], part[3][:, 128:256]),
                ],
                axis=1,
            )
            weight = jnp.concatenate(
                [jnp.where(first, sums[0], sums[1]), jnp.where(first, sums[2], sums[3])], axis=1
            )
            items[i][4]((number / weight).astype(BF16))

        stages = (score, weigh, gather, place_heads)
        for step in range(len(items) + lags[-1]):
            for stage, lag in zip(stages, lags):
                if 0 <= step - lag < len(items):
                    stage(step - lag)

    def mix_fine(m):
        items = []
        for t in range(2):
            for g in range(2):
                rows, near, cols = pl.ds(128 * t, 128), pl.ds(128 * t, 256), pl.ds(g * G, G)

                def put(value, rows=rows, cols=cols):
                    mix[m, rows, cols] = value

                items.append(
                    (
                        lambda g=g, rows=rows: q_s[2 * m + g, rows, :],
                        lambda g=g, near=near: k_s[2 * m + g, near, :],
                        lambda g=g, near=near: v_s[2 * m + g, near, :],
                        lambda t=t: fmask[t],
                        put,
                    )
                )
        attend(items, (0, 1, 1, 2))

    def add_fine(m):
        update = dot_nn(mix[m], w[3 * FI : 4 * FI, :])
        x[m, 2:10] += update.reshape(8, 2, 2, 8, D)

    def coarse_jobs(first, count, parts):
        jobs = []
        for part in parts:
            for g in range(CI // G):
                at = part * CI + g * G

                def put(block, part=part, g=g):
                    (q_s, k_s, v_s)[part][g, 0:count, :] = block

                jobs.append(
                    (lambda at=at: dot_nn(nrm[first : first + count, :], wt[:, at : at + G]), part, g, put)
                )
        return jobs

    def coarse_queries(m):
        nrm[32:96, :] = normed(cin[m, 32:96, :].astype(F32), m)
        run_jobs(coarse_jobs(32, COWN, (0,)))

    def coarse_rest(m):
        for i in range(2):
            edge = edge_in[m, i].astype(F32)
            edge = jnp.concatenate([edge[0:24], edge[24:48]], axis=1)
            at = (8, 96)[i]
            nrm[at : at + 24, :] = normed(edge, m)
        run_jobs(coarse_jobs(0, COARSE, (1, 2)))
        items = []
        for g in range(6):

            def put(value, g=g):
                grp[:, g * G : (g + 1) * G] = value

            items.append(
                (
                    lambda g=g: q_s[g, 0:COWN, :],
                    lambda g=g: k_s[g, 0:COARSE, :],
                    lambda g=g: v_s[g, 0:COARSE, :],
                    lambda: cmask[...],
                    put,
                )
            )
        attend(items, (0, 1, 2, 3))
        update = dot_nn(grp[:, 0:CI], w[3 * CI : 4 * CI, :])
        put_coarse(m, cin[m, 32:96, :].astype(F32) + update)

    def put_coarse(m, result):
        cout[m] = result.astype(BF16)
        for i in range(2):
            rows = result[0:24] if i == 0 else result[40:64]
            edge_out[m, i] = jnp.concatenate([rows[:, 0:512], rows[:, 512:1024]], axis=0).astype(BF16)

    def merge(m):
        own = x[m, 2:10]
        for a in range(2):
            for c in range(2):
                at = (2 * a + c) * D
                grp[:, at : at + D] = own[:, a, c].reshape(COWN, D).astype(BF16)
        put_coarse(m, dot_nn(grp[...], w[4 * FI :, :]))

    def head(m):
        top = x[m, 2:10].reshape(OWN, D)
        scale = lax.rsqrt(jnp.mean(top * top, axis=-1, keepdims=True) + EPS)
        pixels = dot_nn((top * scale).astype(BF16), pox[...])
        token = iota((16, 256), 0)
        col = iota((16, 256), 1)
        own = 2 * (token % 8) + token // 8 == 4 * (col // 64) + (col // 4) % 4
        spread = jnp.where(own[None], pixels.reshape(16, 16, 256), 0.0)
        total = jnp.sum(spread, axis=1)
        pixout[m, 0] = total[:, 0:128]
        pixout[m, 1] = total[:, 128:256]

    def coarse_own(m, seg):
        return remote(cout.at[m], cin.at[m, pl.ds(32, 64), :], c_s.at[m, 0], c_r.at[m, 0], seg + 1, b)

    def edge_up(m, seg):
        if seg < 2:
            src, dst = edge_out.at[m, 0], edge_in.at[m, 1]
        else:
            src, dst = cout.at[m, pl.ds(0, 16), :], cin.at[m, pl.ds(96, 16), :]
        return remote(src, dst, c_s.at[m, 1], c_r.at[m, 2], seg + 1, b - 1)

    def edge_down(m, seg):
        if seg < 2:
            src, dst = edge_out.at[m, 1], edge_in.at[m, 0]
        else:
            src, dst = cout.at[m, pl.ds(48, 16), :], cin.at[m, pl.ds(16, 16), :]
        return remote(src, dst, c_s.at[m, 2], c_r.at[m, 1], seg + 1, b + 1)

    def send_coarse(m, seg, act):
        act(coarse_own(m, seg))

        @pl.when(has_up)
        def _():
            act(edge_up(m, seg))

        @pl.when(has_down)
        def _():
            act(edge_down(m, seg))

    def take_own(m):
        arrived(cin.at[m, pl.ds(32, 64), :], c_r.at[m, 0])

    def take_edges(m, above, below):
        @pl.when(has_up)
        def _():
            arrived(above, c_r.at[m, 1])

        @pl.when(has_down)
        def _():
            arrived(below, c_r.at[m, 2])

    def pixels_on():
        return remote(xs, xs, xs_s, xs_r, 3, b)

    def half(which):
        return wo.at[pl.ds(pl.multiple_of(which * 256, 256), 256), :]

    mine, other = b % 2, 1 - b % 2

    def half_copy():
        rows = pl.ds(pl.multiple_of(3 * FI + mine * 256, 256), 256)
        return pltpu.make_async_copy(w_hbm.at[0, rows, :], half(mine), in_sem.at[6])

    def weights_on(seg):
        return remote(half(mine), half(mine), wo_s, wo_r, seg, b)

    def weights_across():
        return remote(half(mine), half(mine), wx_s, wx_r, 3, b + 1 - 2 * mine)

    def mix_copy(m):
        return remote(mix.at[m], mixed.at[m, pl.ds(64, OWN), :], mix_s.at[m], mix_r.at[m], 3, b)

    def mix_up(m):
        return remote(
            mixed.at[m, pl.ds(64, 64), :], mixed.at[m, pl.ds(320, 64), :], fwd_s.at[m, 0], fwd_r.at[m, 1], 3, b - 1
        )

    def mix_down(m):
        return remote(
            mixed.at[m, pl.ds(256, 64), :], mixed.at[m, pl.ds(0, 64), :], fwd_s.at[m, 1], fwd_r.at[m, 0], 3, b + 1
        )

    def forward_mix(m, act):
        @pl.when(has_up)
        def _():
            act(mix_up(m))

        @pl.when(has_down)
        def _():
            act(mix_down(m))

    def pixel_copy(m, seg):
        return pltpu.make_async_remote_copy(
            src_ref=pixout.at[m, seg // 2], dst_ref=pixin.at[m], send_sem=pix_s.at[m, seg], recv_sem=pix_r.at[m],
            device_id=(seg, b), device_id_type=pl.DeviceIdType.MESH,
        )

    def start(copy):
        copy.start()

    def sent(copy):
        copy.wait_send()

    def take_gains():
        freq_copy.wait()
        cond_copy.wait()
        make_gains()

    @pl.when(s == 0)
    def _():
        frame_copy.wait()
        noise_copy.wait()
        scale_pixels()
        pl.semaphore_wait(barrier, 2 + 2 * edges)

        @pl.when(has_up)
        def _():
            halo_up().start()

        @pl.when(has_down)
        def _():
            halo_down().start()

        half_copy().start()
        make_fine_links()
        link_copy(3).start()
        take_gains()
        patch_in_copy.wait()
        make_embedding()
        embed_own(0)
        half_copy().wait()
        weights_on(1).start()
        weight_copy(0).wait()
        for i in range(1, CHUNKS):
            weight_copy(i).start()
        project_own(0)
        make_fine_mask()

        @pl.when(has_up)
        def _():
            arrived(xs.at[:, pl.ds(0, 16), :], halo_r.at[0])

        @pl.when(has_down)
        def _():
            arrived(xs.at[:, pl.ds(80, 16), :], halo_r.at[1])

        pixels_on().start()
        for m in range(MB):
            if m > 0:
                embed_own(m)
                project_own(m)
            project_halo(m)
            mix_fine(m)
            if m == 0:
                for i in range(1, CHUNKS):
                    weight_copy(i).wait()
            add_fine(m)
            merge(m)
            send_coarse(m, 0, start)
            mix_copy(m).start()

    @pl.when((s == 1) | (s == 2))
    def _():
        nrm[0:8, :] = jnp.zeros((8, D), BF16)
        nrm[120:128, :] = jnp.zeros((8, D), BF16)

        @pl.when(b == 0)
        def _():
            edge_in[:, 0] = jnp.zeros((MB, 48, 512), BF16)

        @pl.when(b == n_space - 1)
        def _():
            edge_in[:, 1] = jnp.zeros((MB, 48, 512), BF16)

        @pl.when(s == 1)
        def _():
            make_coarse_links()
            pl.semaphore_wait(barrier, 2 + edges)
            link_copy(2).start()
            arrived(half(mine), wo_r)
            weights_on(3).start()

        @pl.when(s == 2)
        def _():
            pl.semaphore_wait(barrier, 1 + edges)
            arrived(links, link_r)

        make_coarse_mask()
        take_gains()
        for i in range(3):
            weight_copy(i).wait()
            transpose_weights(6 * i, 6 * i + 6, 0)
        weight_copy(3).wait()

        def one_batch(m, carry):
            take_own(m)
            coarse_queries(m)
            take_edges(m, edge_in.at[m, 0], edge_in.at[m, 1])
            coarse_rest(m)

            @pl.when(s == 1)
            def _():
                send_coarse(m, 1, start)

            @pl.when(s == 2)
            def _():
                send_coarse(m, 2, start)

            return carry

        lax.fori_loop(0, MB, one_batch, 0)

    @pl.when(s == 3)
    def _():
        @pl.when(b == 0)
        def _():
            cin[:, 16:32, :] = jnp.zeros((MB, 16, D), BF16)
            mixed[:, 0:64, :] = jnp.zeros((MB, 64, FI), BF16)

        @pl.when(b == n_space - 1)
        def _():
            cin[:, 96:112, :] = jnp.zeros((MB, 16, D), BF16)
            mixed[:, 320:384, :] = jnp.zeros((MB, 64, FI), BF16)

        take_gains()
        patch_in_copy.wait()
        make_embedding()
        patch_out_copy.wait()
        entry = iota((16, 256), 0)
        col = iota((16, 256), 1)
        pick = (entry == 4 * ((col // 16) % 4) + col % 4).astype(BF16)
        pox[...] = lax.dot_general(
            patch_out[...], pick, (((0,), (0,)), ((), ())), preferred_element_type=F32
        ).astype(BF16)
        weight_copy(0).wait()
        weight_copy(1).wait()
        transpose_weights(8, 12, 8)
        weight_copy(2).wait()
        transpose_weights(12, 18, 8)
        weight_copy(3).wait()
        transpose_weights(18, 24, 8)
        pl.semaphore_wait(barrier, 4 + edges)
        arrived(links, link_r)
        make_fine_mask()
        arrived(half(mine), wo_r)
        weights_across().start()
        arrived(xs, xs_r)
        for m in range(MB):
            embed_all(m)
        arrived(half(other), wx_r)
        for m in range(MB):
            arrived(mixed.at[m, pl.ds(64, OWN), :], mix_r.at[m])
            forward_mix(m, start)

        def one_batch(m, carry):
            @pl.when(has_up)
            def _():
                arrived(mixed.at[m, pl.ds(0, 64), :], fwd_r.at[m, 0])

            @pl.when(has_down)
            def _():
                arrived(mixed.at[m, pl.ds(320, 64), :], fwd_r.at[m, 1])

            make_skip(m)
            take_own(m)
            take_edges(m, cin.at[m, pl.ds(16, 16), :], cin.at[m, pl.ds(96, 16), :])
            widen(m)
            project_fine(m)
            mix_fine(m)
            add_fine(m)
            head(m)
            for seg in range(4):
                pixel_copy(m, seg).start()
            return carry

        lax.fori_loop(0, MB, one_batch, 0)

    for m in range(MB):
        arrived(pixin.at[m], pix_r.at[m])
        pixels = pixin[m]
        pixels = jnp.where(s % 2 == 1, pltpu.roll(pixels, 64, 1), pixels)
        for a in range(4):
            placed[pl.ds(a, 16, stride=4), :] = pltpu.roll(pixels, (128 - 16 * a) % 128, 1)
        out[m] = placed[...].T[0:16, :]

    @pl.when(s == 0)
    def _():
        @pl.when(has_up)
        def _():
            halo_up().wait_send()

        @pl.when(has_down)
        def _():
            halo_down().wait_send()

        link_copy(3).wait_send()
        for m in range(MB):
            send_coarse(m, 0, sent)
            mix_copy(m).wait_send()
        weights_on(1).wait_send()
        pixels_on().wait_send()

    @pl.when(s == 1)
    def _():
        link_copy(2).wait_send()
        weights_on(3).wait_send()
        for m in range(MB):
            send_coarse(m, 1, sent)

    @pl.when(s == 2)
    def _():
        for m in range(MB):
            send_coarse(m, 2, sent)

    @pl.when(s == 3)
    def _():
        weights_across().wait_send()
        for m in range(MB):
            forward_mix(m, sent)
            for seg in range(4):
                pixel_copy(m, seg).wait_send()


def per_device(
    clean_frames, noise, noise_steps, noise_freqs, cond_weights, patch_in, patch_out, section_weights, head_scales,
    fine_links, coarse_links,
):
    vmem = pl.BlockSpec(memory_space=pltpu.VMEM)
    smem = pl.BlockSpec(memory_space=pltpu.SMEM)
    hbm = pl.BlockSpec(memory_space=pl.ANY)
    dma = pltpu.SemaphoreType.DMA
    placed = pl.pallas_call(
        functools.partial(kernel, lax.axis_size("space")),
        out_shape=jax.ShapeDtypeStruct((MB, 16, 64), F32),
        in_specs=[hbm, hbm, smem, hbm, hbm, hbm, hbm, hbm, smem, smem, smem],
        out_specs=vmem,
        scratch_shapes=[
            pltpu.VMEM((6144, D), BF16),
            pltpu.VMEM((D, 3 * CI), BF16),
            pltpu.VMEM((MB, 64, 64), F32),
            pltpu.VMEM((MB, 64, 64), F32),
            pltpu.VMEM((128,), F32),
            pltpu.VMEM((1, 256, D), BF16),
            pltpu.VMEM((16, D), F32),
            pltpu.VMEM((16, D), BF16),
            pltpu.VMEM((MB, 96, 128), F32),
            pltpu.VMEM((MB, 12, 2, 2, 8, D), F32),
            pltpu.VMEM((2 * OWN, D), BF16),
            pltpu.VMEM((128, D), BF16),
            pltpu.VMEM((6, OWN, G), BF16),
            pltpu.VMEM((6, FINE, G), BF16),
            pltpu.VMEM((6, FINE, G), BF16),
            pltpu.VMEM((MB, OWN, FI), BF16),
            pltpu.VMEM((MB, FINE, FI), BF16),
            pltpu.VMEM((COWN, 4 * D), BF16),
            pltpu.VMEM((FI, D), BF16),
            pltpu.VMEM((MB, COARSE, D), BF16),
            pltpu.VMEM((MB, COWN, D), BF16),
            pltpu.VMEM((MB, 2, 48, 512), BF16),
            pltpu.VMEM((MB, 2, 48, 512), BF16),
            pltpu.VMEM((768, D), BF16),
            pltpu.VMEM((D, 256), BF16),
            pltpu.VMEM((8, D), F32),
            pltpu.VMEM((8, G), F32),
            pltpu.VMEM((8, 256), F32),
            pltpu.VMEM((2, 128, 256), BF16),
            pltpu.VMEM((64, 128), BF16),
            pltpu.VMEM((MB, 2, 16, 128), F32),
            pltpu.VMEM((MB, 16, 128), F32),
            pltpu.VMEM((64, 128), F32),
            dma((CHUNKS,)),
            dma((7,)),
            dma((2,)), dma((2,)),
            dma(()), dma(()),
            dma((MB, 3)), dma((MB, 3)),
            dma(()), dma(()),
            dma(()), dma(()),
            dma(()), dma(()),
            dma((MB,)), dma((MB,)),
            dma((MB, 2)), dma((MB, 2)),
            dma((MB, 4)), dma((MB,)),
        ],
        compiler_params=pltpu.CompilerParams(
            collective_id=0, has_side_effects=True, vmem_limit_bytes=58 << 20
        ),
    )(
        clean_frames, noise, noise_steps, noise_freqs, cond_weights, patch_in, patch_out.T, section_weights,
        head_scales, fine_links, coarse_links,
    )
    return placed.transpose(0, 2, 1)


def solution(mesh):
    in_specs = (
        P(None, "space", None),
        P(None, "space", None),
        P(),
        P(),
        P("segment", None, None),
        P(),
        P(),
        P("segment", None, None),
        P("segment", None),
        P("space", None, None),
        P("space", None, None),
    )
    out_specs = P(None, "space", "segment")
    return jax.shard_map(
        per_device, mesh=mesh, in_specs=in_specs, out_specs=out_specs, check_vma=False
    )
```

```python
import functools
import math

import jax
import jax.numpy as jnp
from jax import lax
from jax.experimental import pallas as pl
from jax.experimental.pallas import tpu as pltpu
from jax.sharding import PartitionSpec as P

STEPS = 1000
MB = 2
D = 1024
FI = 512
CI = 1536
G = 256
OWN = 256
FINE = 384
COWN = 64
COARSE = 128
EPS = 1e-06

LOG_LOW = math.log(0.002)
LOG_HIGH = math.log(80.0)
LOG2E = 1.0 / math.log(2.0)

F32 = jnp.float32
BF16 = jnp.bfloat16
NT = (((1,), (1,)), ((), ()))
NN = (((1,), (0,)), ((), ()))

CHUNK = 1536
CHUNKS = 4


def dot_nt(a, b):
    return lax.dot_general(a, b, NT, preferred_element_type=F32)


def dot_nn(a, b):
    return lax.dot_general(a, b, NN, preferred_element_type=F32)


def iota(shape, dim):
    return lax.broadcasted_iota(jnp.int32, shape, dim)


def split3(value):
    hi = value.astype(BF16)
    rest = value - hi.astype(F32)
    mid = rest.astype(BF16)
    return hi, mid, (rest - mid.astype(F32)).astype(BF16)


def kernel(
    n_space,
    frames_hbm, noise_hbm, steps, freqs_hbm, cond_hbm, patch_in_hbm, patch_out_hbm, w_hbm, scales, fine_links,
    coarse_links,
    out,
    w, wt, frames, noise, freqs, cond, patch_in, patch_out, xs, x, nrm, halo, q_s, k_s, v_s, mix, mixed, grp, wo, cin, cout,
    edge_out, edge_in, w3, pox, gains, qscale, links, fmask, cmask, pixout, pixin, placed,
    w_sem, in_sem, halo_s, halo_r, link_s, link_r, c_s, c_r, xs_s, xs_r, wo_s, wo_r, wx_s, wx_r, mix_s, mix_r, fwd_s,
    fwd_r, pix_s, pix_r,
):
    s = lax.axis_index("segment")
    p = lax.axis_index("space")
    b = p + (s // 2) * (1 - 2 * (p % 2))
    has_up = b > 0
    has_down = b < n_space - 1

    def place(seg, block):
        return block + (seg // 2) * (1 - 2 * (block % 2))

    def remote(src, dst, ssem, rsem, seg, block):
        return pltpu.make_async_remote_copy(
            src_ref=src, dst_ref=dst, send_sem=ssem, recv_sem=rsem,
            device_id=(seg, place(seg, block)), device_id_type=pl.DeviceIdType.MESH,
        )

    def arrived(dst, rsem):
        pltpu.make_async_remote_copy(
            src_ref=dst, dst_ref=dst, send_sem=rsem, recv_sem=rsem,
            device_id=(s, p), device_id_type=pl.DeviceIdType.MESH,
        ).wait_recv()

    def weight_copy(i):
        rows = pl.ds(i * CHUNK, CHUNK)
        return pltpu.make_async_copy(w_hbm.at[0, rows, :], w.at[rows, :], w_sem.at[i])

    freq_copy = pltpu.make_async_copy(freqs_hbm, freqs, in_sem.at[0])
    cond_copy = pltpu.make_async_copy(cond_hbm, cond, in_sem.at[1])
    frame_copy = pltpu.make_async_copy(frames_hbm, frames, in_sem.at[2])
    noise_copy = pltpu.make_async_copy(noise_hbm, noise, in_sem.at[3])
    patch_in_copy = pltpu.make_async_copy(patch_in_hbm, patch_in, in_sem.at[4])
    patch_out_copy = pltpu.make_async_copy(patch_out_hbm, patch_out, in_sem.at[5])

    barrier = pltpu.get_barrier_semaphore()

    def greet(seg, space):
        pl.semaphore_signal(barrier, inc=1, device_id=(seg, space), device_id_type=pl.DeviceIdType.MESH)

    @pl.when((s == 0) | (s == 3))
    def _():
        @pl.when(has_up)
        def _():
            greet(s, place(s, b - 1))

        @pl.when(has_down)
        def _():
            greet(s, place(s, b + 1))

    @pl.when(s == 0)
    def _():
        frame_copy.start()
        noise_copy.start()

    @pl.when((s == 0) | (s == 3))
    def _():
        patch_in_copy.start()

    freq_copy.start()
    cond_copy.start()
    weight_copy(0).start()

    @pl.when(s > 0)
    def _():
        for i in range(1, CHUNKS):
            weight_copy(i).start()

    greet(3, place(3, p))

    @pl.when(s > 0)
    def _():
        greet(s - 1, place(s - 1, b))

        @pl.when(has_up)
        def _():
            greet(s - 1, place(s - 1, b - 1))

        @pl.when(has_down)
        def _():
            greet(s - 1, place(s - 1, b + 1))

    @pl.when(s == 3)
    def _():
        greet(0, b)
        greet(1, b)
        patch_out_copy.start()

    def level_row(m):
        step = jnp.full((1, 128), steps[m], jnp.int32).astype(F32)
        return jnp.exp(LOG_LOW + step / (STEPS - 1) * (LOG_HIGH - LOG_LOW))

    lane = iota((1, G), 1) // 64
    for g in range(6):
        four = [scales[0, 4 * g + h] for h in range(4)]
        row = jnp.where(lane == 0, four[0], jnp.where(lane == 1, four[1], jnp.where(lane == 2, four[2], four[3])))
        qscale[g : g + 1, :] = row * (LOG2E / 64.0)

    head_mean = jnp.where(iota((G, G), 0) // 64 == iota((G, G), 1) // 64, 1.0 / 64.0, 0.0).astype(BF16)

    def make_gains():
        rows = []
        for m in range(MB):
            phases = 2.0 * math.pi * (jnp.log(level_row(m)) / 4.0) * freqs[...].reshape(1, 128)
            rows.append(jnp.concatenate([jnp.cos(phases), jnp.sin(phases)], axis=1))
        features = jnp.concatenate(rows + [jnp.zeros((6, 256), F32)], axis=0)
        hi, mid, low = split3(features)
        gains[...] = 1.0 + (dot_nn(hi, cond[0]) + dot_nn(mid, cond[0]) + dot_nn(low, cond[0]))

    def make_fine_mask():
        query = iota((128, 256), 0)
        key = iota((128, 256), 1)
        row_gap = key // 16 - 4 - query // 16
        query_col = 2 * (query % 8) + (query // 8) % 2
        key_col = 2 * (key % 8) + (key // 8) % 2
        col_gap = key_col - query_col
        near = (row_gap <= 3) & (row_gap >= -3) & (col_gap <= 3) & (col_gap >= -3)
        for t in range(2):
            left = jnp.broadcast_to(links[2 * t : 2 * t + 1, :], (128, 256))
            right = jnp.broadcast_to(links[2 * t + 1 : 2 * t + 2, :], (128, 256))
            value = jnp.where(query_col < 8, left, right)
            fmask[t] = jnp.where(near, value, 0.0).astype(BF16)

    def make_coarse_mask():
        query = iota((64, 128), 0)
        key = iota((64, 128), 1)
        row_gap = key // 8 - 4 - query // 8
        col_gap = key % 8 - query % 8
        near = (row_gap <= 3) & (row_gap >= -3) & (col_gap <= 3) & (col_gap >= -3)
        value = jnp.broadcast_to(links[0:1, 0:128], (64, 128))
        cmask[...] = jnp.where(near, value, 0.0).astype(BF16)

    def make_fine_links():
        key = iota((1, 256), 1)
        key_row = key // 16
        key_tile = (key % 8) // 4
        for t in range(2):
            for c in range(2):
                row = jnp.zeros((1, 256), F32)
                for dy in range(3):
                    in_row = (key_row >= (0, 4, 12)[dy]) & (key_row < (4, 12, 16)[dy])
                    for kc in range(2):
                        link = fine_links[t, c, 3 * dy + kc - c + 1].astype(F32)
                        row = jnp.where(in_row & (key_tile == kc), link, row)
                links[2 * t + c : 2 * t + c + 1, :] = row

    def make_coarse_links():
        key_row = iota((1, 256), 1) // 8
        row = jnp.zeros((1, 256), F32)
        for dy in range(3):
            in_row = (key_row >= (0, 4, 12)[dy]) & (key_row < (4, 12, 16)[dy])
            row = jnp.where(in_row, coarse_links[0, 0, 3 * dy + 1].astype(F32), row)
        links[0:1, :] = row

    def halo_up():
        return remote(xs.at[:, pl.ds(16, 16), :], xs.at[:, pl.ds(80, 16), :], halo_s.at[0], halo_r.at[1], 0, b - 1)

    def halo_down():
        return remote(xs.at[:, pl.ds(64, 16), :], xs.at[:, pl.ds(0, 16), :], halo_s.at[1], halo_r.at[0], 0, b + 1)

    def link_copy(seg):
        return remote(links, links, link_s, link_r, seg, b)

    edges = has_up.astype(jnp.int32) + has_down.astype(jnp.int32)

    def scale_pixels():
        for m in range(MB):
            level = level_row(m)[:, 0:64]
            scaled = (frames[m] + level * noise[m]) * lax.rsqrt(level * level + 0.25)
            xs[m, 16:80, :] = jnp.concatenate([scaled, jnp.zeros((64, 64), F32)], axis=1)

        @pl.when(b == 0)
        def _():
            xs[:, 0:16, :] = jnp.zeros((MB, 16, 128), F32)

        @pl.when(b == n_space - 1)
        def _():
            xs[:, 80:96, :] = jnp.zeros((MB, 16, 128), F32)

    def make_embedding():
        entry = iota((256, 16), 0)
        pick = (iota((256, 16), 1) == 4 * (entry // 64) + entry % 4).astype(BF16)
        hi, low, _ = split3(patch_in[...])
        wide = dot_nn(pick, hi).astype(BF16)
        w3[0:256, :] = wide
        w3[256:512, :] = dot_nn(pick, low).astype(BF16)
        w3[512:768, :] = wide

    def transpose_weights(first, last, base):
        eye = (iota((G, G), 0) == iota((G, G), 1)).astype(BF16)

        def tile(i, carry):
            row = pl.multiple_of(i * G, G)
            col = pl.multiple_of((i - base) * G, G)
            for k in range(D // G):
                block = dot_nt(eye, w[pl.ds(row, G), k * G : (k + 1) * G])
                wt[k * G : (k + 1) * G, pl.ds(col, G)] = block.astype(BF16)
            return carry

        lax.fori_loop(first, last, tile, 0)

    def normed(value, m):
        scale = lax.rsqrt(jnp.mean(value * value, axis=-1, keepdims=True) + EPS)
        return (value * scale * gains[pl.ds(m, 1), :]).astype(BF16)

    def embed(rows4):
        flat = jnp.concatenate(
            [rows4[0] + pltpu.roll(rows4[1], 64, 1), rows4[2] + pltpu.roll(rows4[3], 64, 1)], axis=1
        )
        hi, low, _ = split3(flat)
        token = iota((16, 256), 0)
        col = iota((16, 256), 1)
        own = ((col % 64) // 4 == 2 * (token % 8) + token // 8).astype(F32)
        count = flat.shape[0]

        def spread(piece):
            wide = jnp.broadcast_to(piece.astype(F32)[:, None, :], (count, 16, 256)) * own[None]
            return wide.reshape(count * 16, 256).astype(BF16)

        first = spread(hi)
        return dot_nn(jnp.concatenate([first, first, spread(low)], axis=1), w3[...])

    def run_jobs(jobs):
        def finish(block, part, g, put):
            if part < 2:
                power = dot_nn((block * block).astype(BF16), head_mean)
                block = block * lax.rsqrt(power + EPS)
            if part == 0:
                block = block * qscale[g : g + 1, :]
            put(block.astype(BF16))

        pending = []
        for make, part, g, put in jobs:
            pending.append((make(), part, g, put))
            if len(pending) > 2:
                finish(*pending.pop(0))
        for job in pending:
            finish(*job)

    def fine_jobs(source, first, count, parts, put):
        jobs = []
        for part in parts:
            for g in range(FI // G):
                at = part * FI + g * G
                lo, n = (first, count) if part == 0 else (0, source.shape[0])
                jobs.append(
                    (
                        lambda at=at, lo=lo, n=n: dot_nt(source[lo : lo + n, :], w[at : at + G, :]),
                        part, g, functools.partial(put, part, g),
                    )
                )
        return jobs

    def embed_own(m):
        own = embed([xs[m, pl.ds(16 + a, 16, stride=4), :] for a in range(4)])
        x[m, 2:10] = own.reshape(8, 2, 2, 8, D)
        nrm[m * OWN : (m + 1) * OWN, :] = normed(own, m)

    def project_own(m):
        def put(part, g, block):
            if part == 0:
                q_s[2 * m + g, :, :] = block
            else:
                (k_s if part == 1 else v_s)[2 * m + g, 64:320, :] = block

        own = nrm.at[pl.ds(pl.multiple_of(m * OWN, OWN), OWN), :]
        run_jobs(fine_jobs(own, 0, OWN, (0, 1, 2), put))

    def project_halo(m):
        rows4 = [
            jnp.concatenate([xs[m, pl.ds(a, 4, stride=4), :], xs[m, pl.ds(80 + a, 4, stride=4), :]], axis=0)
            for a in range(4)
        ]
        halo[...] = normed(embed(rows4), m)

        def put(part, g, block):
            dst = k_s if part == 1 else v_s
            dst[2 * m + g, 0:64, :] = block[0:64]
            dst[2 * m + g, 320:384, :] = block[64:128]

        run_jobs(fine_jobs(halo, 0, 128, (1, 2), put))

    def widen(m):
        coarse = cin[m, 16:112, :]
        for a in range(2):
            for c in range(2):
                at = (2 * a + c) * D
                x[m, :, a, c] += dot_nn(coarse, wt[:, at : at + D]).reshape(12, 8, D)

    def embed_all(m):
        embedded = embed([xs[m, pl.ds(a, 24, stride=4), :] for a in range(4)])
        x[m] = embedded.reshape(12, 2, 2, 8, D)

    def make_skip(m):
        whole = (x[m].reshape(FINE, D) + dot_nn(mixed[m], wo[...])).astype(BF16)
        x[m] = whole.astype(F32).reshape(12, 2, 2, 8, D)

    def project_fine(m):
        nrm[0:FINE, :] = normed(x[m].reshape(FINE, D), m)

        def put(part, g, block):
            (q_s, k_s, v_s)[part][2 * m + g, :, :] = block

        run_jobs(fine_jobs(nrm.at[0:FINE], 64, OWN, (0, 1, 2), put))

    def attend(items, lags):
        held = [{} for _ in items]

        def score(i):
            queries, keys = items[i][0](), items[i][1]()
            head = iota(queries.shape, 1) // 64
            stacked = jnp.concatenate(
                [jnp.where(head == h, queries, jnp.zeros_like(queries)) for h in range(4)], axis=0
            )
            held[i]["score"] = dot_nt(stacked, keys)

        def weigh(i):
            expo = jnp.exp2(held[i].pop("score")).astype(BF16)
            held[i]["expo"] = expo * jnp.concatenate([items[i][3]()] * 4, axis=0)

        def gather(i):
            expo = held[i].pop("expo")
            held[i]["sum"] = jnp.sum(expo.astype(F32), axis=-1, keepdims=True)
            held[i]["mixed"] = dot_nn(expo, items[i][2]())

        def place_heads(i):
            total, value = held[i].pop("sum"), held[i].pop("mixed")
            count = value.shape[0] // 4
            part = [value[h * count : (h + 1) * count] for h in range(4)]
            sums = [total[h * count : (h + 1) * count] for h in range(4)]
            first = iota((count, 128), 1) < 64
            number = jnp.concatenate(
                [
                    jnp.where(first, part[0][:, 0:128], part[1][:, 0:128]),
                    jnp.where(first, part[2][:, 128:256], part[3][:, 128:256]),
                ],
                axis=1,
            )
            weight = jnp.concatenate(
                [jnp.where(first, sums[0], sums[1]), jnp.where(first, sums[2], sums[3])], axis=1
            )
            items[i][4]((number / weight).astype(BF16))

        stages = (score, weigh, gather, place_heads)
        for step in range(len(items) + lags[-1]):
            for stage, lag in zip(stages, lags):
                if 0 <= step - lag < len(items):
                    stage(step - lag)

    def mix_fine(m):
        items = []
        for t in range(2):
            for g in range(2):
                rows, near, cols = pl.ds(128 * t, 128), pl.ds(128 * t, 256), pl.ds(g * G, G)

                def put(value, rows=rows, cols=cols):
                    mix[m, rows, cols] = value

                items.append(
                    (
                        lambda g=g, rows=rows: q_s[2 * m + g, rows, :],
                        lambda g=g, near=near: k_s[2 * m + g, near, :],
                        lambda g=g, near=near: v_s[2 * m + g, near, :],
                        lambda t=t: fmask[t],
                        put,
                    )
                )
        attend(items, (0, 1, 1, 2))

    def add_fine(m):
        update = dot_nn(mix[m], w[3 * FI : 4 * FI, :])
        x[m, 2:10] += update.reshape(8, 2, 2, 8, D)

    def coarse_jobs(first, count, parts):
        jobs = []
        for part in parts:
            for g in range(CI // G):
                at = part * CI + g * G

                def put(block, part=part, g=g):
                    (q_s, k_s, v_s)[part][g, 0:count, :] = block

                jobs.append(
                    (lambda at=at: dot_nn(nrm[first : first + count, :], wt[:, at : at + G]), part, g, put)
                )
        return jobs

    def coarse_queries(m):
        nrm[32:96, :] = normed(cin[m, 32:96, :].astype(F32), m)
        run_jobs(coarse_jobs(32, COWN, (0,)))

    def coarse_rest(m):
        for i in range(2):
            edge = edge_in[m, i].astype(F32)
            edge = jnp.concatenate([edge[0:24], edge[24:48]], axis=1)
            at = (8, 96)[i]
            nrm[at : at + 24, :] = normed(edge, m)
        run_jobs(coarse_jobs(0, COARSE, (1, 2)))
        items = []
        for g in range(6):

            def put(value, g=g):
                grp[:, g * G : (g + 1) * G] = value

            items.append(
                (
                    lambda g=g: q_s[g, 0:COWN, :],
                    lambda g=g: k_s[g, 0:COARSE, :],
                    lambda g=g: v_s[g, 0:COARSE, :],
                    lambda: cmask[...],
                    put,
                )
            )
        attend(items, (0, 1, 2, 3))
        update = dot_nn(grp[:, 0:CI], w[3 * CI : 4 * CI, :])
        put_coarse(m, cin[m, 32:96, :].astype(F32) + update)

    def put_coarse(m, result):
        cout[m] = result.astype(BF16)
        for i in range(2):
            rows = result[0:24] if i == 0 else result[40:64]
            edge_out[m, i] = jnp.concatenate([rows[:, 0:512], rows[:, 512:1024]], axis=0).astype(BF16)

    def merge(m):
        own = x[m, 2:10]
        for a in range(2):
            for c in range(2):
                at = (2 * a + c) * D
                grp[:, at : at + D] = own[:, a, c].reshape(COWN, D).astype(BF16)
        put_coarse(m, dot_nn(grp[...], w[4 * FI :, :]))

    def head(m):
        top = x[m, 2:10].reshape(OWN, D)
        scale = lax.rsqrt(jnp.mean(top * top, axis=-1, keepdims=True) + EPS)
        pixels = dot_nn((top * scale).astype(BF16), pox[...])
        token = iota((16, 256), 0)
        col = iota((16, 256), 1)
        own = 2 * (token % 8) + token // 8 == 4 * (col // 64) + (col // 4) % 4
        spread = jnp.where(own[None], pixels.reshape(16, 16, 256), 0.0)
        total = jnp.sum(spread, axis=1)
        pixout[m, 0] = total[:, 0:128]
        pixout[m, 1] = total[:, 128:256]

    def coarse_own(m, seg):
        return remote(cout.at[m], cin.at[m, pl.ds(32, 64), :], c_s.at[m, 0], c_r.at[m, 0], seg + 1, b)

    def edge_up(m, seg):
        if seg < 2:
            src, dst = edge_out.at[m, 0], edge_in.at[m, 1]
        else:
            src, dst = cout.at[m, pl.ds(0, 16), :], cin.at[m, pl.ds(96, 16), :]
        return remote(src, dst, c_s.at[m, 1], c_r.at[m, 2], seg + 1, b - 1)

    def edge_down(m, seg):
        if seg < 2:
            src, dst = edge_out.at[m, 1], edge_in.at[m, 0]
        else:
            src, dst = cout.at[m, pl.ds(48, 16), :], cin.at[m, pl.ds(16, 16), :]
        return remote(src, dst, c_s.at[m, 2], c_r.at[m, 1], seg + 1, b + 1)

    def send_coarse(m, seg, act):
        if seg < 2:
            act(coarse_own(m, seg))

        @pl.when(has_up)
        def _():
            act(edge_up(m, seg))

        @pl.when(has_down)
        def _():
            act(edge_down(m, seg))

        if seg == 2:
            act(coarse_own(m, seg))

    def take_own(m):
        arrived(cin.at[m, pl.ds(32, 64), :], c_r.at[m, 0])

    def take_edges(m, above, below):
        @pl.when(has_up)
        def _():
            arrived(above, c_r.at[m, 1])

        @pl.when(has_down)
        def _():
            arrived(below, c_r.at[m, 2])

    def pixels_on():
        return remote(xs, xs, xs_s, xs_r, 3, b)

    def half(which):
        return wo.at[pl.ds(pl.multiple_of(which * 256, 256), 256), :]

    mine, other = b % 2, 1 - b % 2

    def half_copy():
        rows = pl.ds(pl.multiple_of(3 * FI + mine * 256, 256), 256)
        return pltpu.make_async_copy(w_hbm.at[0, rows, :], half(mine), in_sem.at[6])

    def weights_on(seg):
        return remote(half(mine), half(mine), wo_s, wo_r, seg, b)

    def weights_across():
        return remote(half(mine), half(mine), wx_s, wx_r, 3, b + 1 - 2 * mine)

    def mix_copy(m):
        return remote(mix.at[m], mixed.at[m, pl.ds(64, OWN), :], mix_s.at[m], mix_r.at[m], 3, b)

    def mix_up(m):
        return remote(
            mixed.at[m, pl.ds(64, 64), :], mixed.at[m, pl.ds(320, 64), :], fwd_s.at[m, 0], fwd_r.at[m, 1], 3, b - 1
        )

    def mix_down(m):
        return remote(
            mixed.at[m, pl.ds(256, 64), :], mixed.at[m, pl.ds(0, 64), :], fwd_s.at[m, 1], fwd_r.at[m, 0], 3, b + 1
        )

    def forward_mix(m, act):
        @pl.when(has_up)
        def _():
            act(mix_up(m))

        @pl.when(has_down)
        def _():
            act(mix_down(m))

    def pixel_copy(m, seg):
        return pltpu.make_async_remote_copy(
            src_ref=pixout.at[m, seg // 2], dst_ref=pixin.at[m], send_sem=pix_s.at[m, seg], recv_sem=pix_r.at[m],
            device_id=(seg, b), device_id_type=pl.DeviceIdType.MESH,
        )

    def start(copy):
        copy.start()

    def sent(copy):
        copy.wait_send()

    def take_gains():
        freq_copy.wait()
        cond_copy.wait()
        make_gains()

    @pl.when(s == 0)
    def _():
        frame_copy.wait()
        noise_copy.wait()
        scale_pixels()
        pl.semaphore_wait(barrier, 2 + 2 * edges)

        @pl.when(has_up)
        def _():
            halo_up().start()

        @pl.when(has_down)
        def _():
            halo_down().start()

        half_copy().start()
        make_fine_links()
        link_copy(3).start()
        take_gains()
        patch_in_copy.wait()
        make_embedding()
        embed_own(0)
        half_copy().wait()
        weights_on(1).start()
        weight_copy(0).wait()
        for i in range(1, CHUNKS):
            weight_copy(i).start()
        project_own(0)
        make_fine_mask()

        @pl.when(has_up)
        def _():
            arrived(xs.at[:, pl.ds(0, 16), :], halo_r.at[0])

        @pl.when(has_down)
        def _():
            arrived(xs.at[:, pl.ds(80, 16), :], halo_r.at[1])

        pixels_on().start()
        for m in range(MB):
            if m > 0:
                embed_own(m)
                project_own(m)
            project_halo(m)
            mix_fine(m)
            if m == 0:
                for i in range(1, CHUNKS):
                    weight_copy(i).wait()
            add_fine(m)
            merge(m)
            send_coarse(m, 0, start)
            mix_copy(m).start()

    @pl.when((s == 1) | (s == 2))
    def _():
        nrm[0:8, :] = jnp.zeros((8, D), BF16)
        nrm[120:128, :] = jnp.zeros((8, D), BF16)

        @pl.when(b == 0)
        def _():
            edge_in[:, 0] = jnp.zeros((MB, 48, 512), BF16)

        @pl.when(b == n_space - 1)
        def _():
            edge_in[:, 1] = jnp.zeros((MB, 48, 512), BF16)

        @pl.when(s == 1)
        def _():
            make_coarse_links()
            pl.semaphore_wait(barrier, 2 + edges)
            link_copy(2).start()
            arrived(half(mine), wo_r)
            weights_on(3).start()

        @pl.when(s == 2)
        def _():
            pl.semaphore_wait(barrier, 1 + edges)
            arrived(links, link_r)

        make_coarse_mask()
        take_gains()
        for i in range(3):
            weight_copy(i).wait()
            transpose_weights(6 * i, 6 * i + 6, 0)
        weight_copy(3).wait()

        def one_batch(m, carry):
            take_own(m)
            coarse_queries(m)
            take_edges(m, edge_in.at[m, 0], edge_in.at[m, 1])
            coarse_rest(m)

            @pl.when(s == 1)
            def _():
                send_coarse(m, 1, start)

            @pl.when(s == 2)
            def _():
                send_coarse(m, 2, start)

            return carry

        lax.fori_loop(0, MB, one_batch, 0)

    @pl.when(s == 3)
    def _():
        @pl.when(b == 0)
        def _():
            cin[:, 16:32, :] = jnp.zeros((MB, 16, D), BF16)
            mixed[:, 0:64, :] = jnp.zeros((MB, 64, FI), BF16)

        @pl.when(b == n_space - 1)
        def _():
            cin[:, 96:112, :] = jnp.zeros((MB, 16, D), BF16)
            mixed[:, 320:384, :] = jnp.zeros((MB, 64, FI), BF16)

        take_gains()
        patch_in_copy.wait()
        make_embedding()
        patch_out_copy.wait()
        entry = iota((16, 256), 0)
        col = iota((16, 256), 1)
        pick = (entry == 4 * ((col // 16) % 4) + col % 4).astype(BF16)
        pox[...] = lax.dot_general(
            patch_out[...], pick, (((0,), (0,)), ((), ())), preferred_element_type=F32
        ).astype(BF16)
        weight_copy(0).wait()
        weight_copy(1).wait()
        transpose_weights(8, 12, 8)
        weight_copy(2).wait()
        transpose_weights(12, 18, 8)
        weight_copy(3).wait()
        transpose_weights(18, 24, 8)
        pl.semaphore_wait(barrier, 4 + edges)
        arrived(links, link_r)
        make_fine_mask()
        arrived(half(mine), wo_r)
        weights_across().start()
        arrived(xs, xs_r)
        for m in range(MB):
            embed_all(m)
        arrived(half(other), wx_r)
        for m in range(MB):
            arrived(mixed.at[m, pl.ds(64, OWN), :], mix_r.at[m])
            forward_mix(m, start)
        for m in range(MB):

            @pl.when(has_up)
            def _():
                arrived(mixed.at[m, pl.ds(0, 64), :], fwd_r.at[m, 0])

            @pl.when(has_down)
            def _():
                arrived(mixed.at[m, pl.ds(320, 64), :], fwd_r.at[m, 1])

            make_skip(m)

        def one_batch(m, carry):
            take_own(m)
            take_edges(m, cin.at[m, pl.ds(16, 16), :], cin.at[m, pl.ds(96, 16), :])
            widen(m)
            project_fine(m)
            mix_fine(m)
            add_fine(m)
            head(m)
            for seg in range(4):
                pixel_copy(m, seg).start()
            return carry

        lax.fori_loop(0, MB, one_batch, 0)

    for m in range(MB):
        arrived(pixin.at[m], pix_r.at[m])
        pixels = pixin[m]
        pixels = jnp.where(s % 2 == 1, pltpu.roll(pixels, 64, 1), pixels)
        for a in range(4):
            placed[pl.ds(a, 16, stride=4), :] = pltpu.roll(pixels, (128 - 16 * a) % 128, 1)
        out[m] = placed[...].T[0:16, :]

    @pl.when(s == 0)
    def _():
        @pl.when(has_up)
        def _():
            halo_up().wait_send()

        @pl.when(has_down)
        def _():
            halo_down().wait_send()

        link_copy(3).wait_send()
        for m in range(MB):
            send_coarse(m, 0, sent)
            mix_copy(m).wait_send()
        weights_on(1).wait_send()
        pixels_on().wait_send()

    @pl.when(s == 1)
    def _():
        link_copy(2).wait_send()
        weights_on(3).wait_send()
        for m in range(MB):
            send_coarse(m, 1, sent)

    @pl.when(s == 2)
    def _():
        for m in range(MB):
            send_coarse(m, 2, sent)

    @pl.when(s == 3)
    def _():
        weights_across().wait_send()
        for m in range(MB):
            forward_mix(m, sent)
            for seg in range(4):
                pixel_copy(m, seg).wait_send()


def per_device(
    clean_frames, noise, noise_steps, noise_freqs, cond_weights, patch_in, patch_out, section_weights, head_scales,
    fine_links, coarse_links,
):
    vmem = pl.BlockSpec(memory_space=pltpu.VMEM)
    smem = pl.BlockSpec(memory_space=pltpu.SMEM)
    hbm = pl.BlockSpec(memory_space=pl.ANY)
    dma = pltpu.SemaphoreType.DMA
    placed = pl.pallas_call(
        functools.partial(kernel, lax.axis_size("space")),
        out_shape=jax.ShapeDtypeStruct((MB, 16, 64), F32),
        in_specs=[hbm, hbm, smem, hbm, hbm, hbm, hbm, hbm, smem, smem, smem],
        out_specs=vmem,
        scratch_shapes=[
            pltpu.VMEM((6144, D), BF16),
            pltpu.VMEM((D, 3 * CI), BF16),
            pltpu.VMEM((MB, 64, 64), F32),
            pltpu.VMEM((MB, 64, 64), F32),
            pltpu.VMEM((128,), F32),
            pltpu.VMEM((1, 256, D), BF16),
            pltpu.VMEM((16, D), F32),
            pltpu.VMEM((16, D), BF16),
            pltpu.VMEM((MB, 96, 128), F32),
            pltpu.VMEM((MB, 12, 2, 2, 8, D), F32),
            pltpu.VMEM((2 * OWN, D), BF16),
            pltpu.VMEM((128, D), BF16),
            pltpu.VMEM((6, OWN, G), BF16),
            pltpu.VMEM((6, FINE, G), BF16),
            pltpu.VMEM((6, FINE, G), BF16),
            pltpu.VMEM((MB, OWN, FI), BF16),
            pltpu.VMEM((MB, FINE, FI), BF16),
            pltpu.VMEM((COWN, 4 * D), BF16),
            pltpu.VMEM((FI, D), BF16),
            pltpu.VMEM((MB, COARSE, D), BF16),
            pltpu.VMEM((MB, COWN, D), BF16),
            pltpu.VMEM((MB, 2, 48, 512), BF16),
            pltpu.VMEM((MB, 2, 48, 512), BF16),
            pltpu.VMEM((768, D), BF16),
            pltpu.VMEM((D, 256), BF16),
            pltpu.VMEM((8, D), F32),
            pltpu.VMEM((8, G), F32),
            pltpu.VMEM((8, 256), F32),
            pltpu.VMEM((2, 128, 256), BF16),
            pltpu.VMEM((64, 128), BF16),
            pltpu.VMEM((MB, 2, 16, 128), F32),
            pltpu.VMEM((MB, 16, 128), F32),
            pltpu.VMEM((64, 128), F32),
            dma((CHUNKS,)),
            dma((7,)),
            dma((2,)), dma((2,)),
            dma(()), dma(()),
            dma((MB, 3)), dma((MB, 3)),
            dma(()), dma(()),
            dma(()), dma(()),
            dma(()), dma(()),
            dma((MB,)), dma((MB,)),
            dma((MB, 2)), dma((MB, 2)),
            dma((MB, 4)), dma((MB,)),
        ],
        compiler_params=pltpu.CompilerParams(
            collective_id=0, has_side_effects=True, vmem_limit_bytes=58 << 20
        ),
    )(
        clean_frames, noise, noise_steps, noise_freqs, cond_weights, patch_in, patch_out.T, section_weights,
        head_scales, fine_links, coarse_links,
    )
    return placed.transpose(0, 2, 1)


def solution(mesh):
    in_specs = (
        P(None, "space", None),
        P(None, "space", None),
        P(),
        P(),
        P("segment", None, None),
        P(),
        P(),
        P("segment", None, None),
        P("segment", None),
        P("space", None, None),
        P("space", None, None),
    )
    out_specs = P(None, "space", "segment")
    return jax.shard_map(
        per_device, mesh=mesh, in_specs=in_specs, out_specs=out_specs, check_vma=False
    )
```
